512 devices in a mesh: section: 16 (over z, y_lo), seq: 32 (over x, y_hi, core).
Axes of the slice: x: 4, y: 8 (y_hi: 4, y_lo: 2; y = y_hi * 2 + y_lo), z: 8, core: 2. Of those that a mesh axis runs over, the one named last changes fastest.
Arguments:
- forward_input: bfloat16 [16, 4096, 1024], P('section', 'seq'), may hold values from -6 to 6
- stored_input: bfloat16 [16, 4096, 1024], P('section', 'seq'), may hold values from -6 to 6
- output_cotangent: bfloat16 [16, 4096, 1024], P('section', 'seq'), may hold values from -6 to 6
- norm_gain: float32 [16, 1024], P('section'), may hold values from 0.5 to 2
- query_weight: bfloat16 [16, 1024, 512], P('section'), may hold values from -0.325 to 0.325
- key_weight: bfloat16 [16, 1024, 128], P('section'), may hold values from -7.3125 to 7.3125
- value_weight: bfloat16 [16, 1024, 128], P('section'), may hold values from -0.1875 to 0.1875
- output_weight: bfloat16 [16, 512, 1024], P('section'), may hold values from -0.25 to 0.25
- frame_index: int32 [4096], replicated, may hold values from 0 to 15, as said below
- valid_counts: int32 [32], replicated, may hold values from 32 to 128
Outputs:
- forward_next: bfloat16 [16, 4096, 1024], P('section', 'seq')
- backward_next: bfloat16 [16, 4096, 1024], P('section', 'seq')
The draws below stay inside these ranges and needn't reach their ends.
Inputs may be any that keep to these rules, and one draw needn't show every extreme that they name: `frame_index`: frame numbers start at 0, never fall along the sequence, and every number up to the largest occurs.
All inputs are finite; a program needn't handle non-finite values.
Results may differ from the reference program's by a relative error of at most 0.028.
The reference program's roundings to bfloat16 on the way count: a program that leaves them out, or rounds other values in their place, can miss the bound.
Values may be sent and summed in bfloat16 or wider, within the bound.
A program may use at most 64 MiB of HBM per device.

```python
import math
from functools import partial
import jax
import jax.numpy as jnp
from jax import lax

D = 1024
HEADS = 8
KV_HEADS = 2
HEAD_DIM = 64
SLICE_TOK = 128
SECTIONS = 16
SLICES = 32
TOKENS = 4096
FRAMES = 16


def weight_pair(base_key):
    spread = 1.3 / D ** 0.5
    query_part = spread * jnp.clip(jax.random.normal(jax.random.fold_in(base_key, 101), (SECTIONS, D, HEADS * HEAD_DIM), jnp.float32), -8.0, 8.0)
    key_part = spread * jnp.clip(jax.random.normal(jax.random.fold_in(base_key, 102), (SECTIONS, D, KV_HEADS * HEAD_DIM), jnp.float32), -8.0, 8.0)
    return (query_part, key_part)


def draw_query_weight(key, part):
    return weight_pair(key)[0].astype(jnp.bfloat16)


def draw_key_weight(key, part):
    return weight_pair(key)[1].astype(jnp.bfloat16)


def draw_frame_index(key, part):
    marks = jax.random.permutation(jax.random.fold_in(key, 201), TOKENS - 1)[:FRAMES - 1] + 1
    position = jnp.arange(TOKENS, dtype=jnp.int32)
    return jnp.sum((position[:, None] >= marks[None, :]).astype(jnp.int32), axis=1).astype(jnp.int32)


def with_ends(values, own_key, least, high):
    spot = [jax.random.randint(jax.random.fold_in(own_key, axis), (), 0, length) for axis, length in enumerate(values.shape)]
    widest = values.shape.index(max(values.shape))
    neighbour = spot[:widest] + [(spot[widest] + 1) % values.shape[widest]] + spot[widest + 1:]
    return values.at[tuple(spot)].set(least).at[tuple(neighbour)].set(high)


def levels(own_key, shape, cuts, least, largest):
    factor_of = 1.0
    for axis_at, blocks in cuts:
        draws = jax.random.uniform(jax.random.fold_in(jax.random.fold_in(own_key, 6), axis_at), (blocks,), jnp.float32, least / len(cuts), largest / len(cuts))
        factor_of = factor_of * jnp.repeat(jnp.exp(draws), shape[axis_at] // blocks).reshape((-1,) + (1,) * (len(shape) - 1 - axis_at))
    return factor_of


def bell_draw(stream_key, shape, scale, most, pieces=(), kind=jnp.bfloat16):
    factor_of = levels(stream_key, shape, pieces, -0.22, 0.18) if pieces else 1.0
    array = jax.random.normal(stream_key, shape, jnp.float32) * scale * factor_of
    return jnp.minimum(jnp.maximum(array, -most), most).astype(kind)


def setup_inputs(seed: int = 0) -> dict:
    seeds = jax.random.split(jax.random.key(seed), 11)
    forward_input = bell_draw(seeds[0], (SECTIONS, TOKENS, D), 1.0, 6.0, ((0, 16), (1, 32)))
    stored_input = bell_draw(seeds[1], (SECTIONS, TOKENS, D), 1.0, 6.0, ((0, 16), (1, 32)))
    output_cotangent = bell_draw(seeds[2], (SECTIONS, TOKENS, D), 1.0, 6.0, ((0, 16), (1, 32)))
    norm_gain = jnp.clip(jnp.exp(math.log(2.0) - 1.3862944 * jax.random.uniform(seeds[3], (SECTIONS, D), jnp.float32) ** levels(seeds[3], (SECTIONS, D), ((0, 16),), -0.2, 0.2)), 0.5, 2.0)
    query_weight = draw_query_weight(jax.random.fold_in(seeds[10], 71), 0)
    key_weight = draw_key_weight(jax.random.fold_in(seeds[10], 71), 0)
    value_weight = bell_draw(seeds[6], (SECTIONS, D, KV_HEADS * HEAD_DIM), D ** -0.5, 0.1875, ((0, 16),))
    output_weight = bell_draw(seeds[7], (SECTIONS, HEADS * HEAD_DIM, D), (HEADS * HEAD_DIM) ** -0.5, 0.25, ((0, 16),))
    frame_index = draw_frame_index(jax.random.fold_in(seeds[10], 71), 0)
    valid_counts = with_ends(jax.random.randint(seeds[9], (SLICES,), SLICE_TOK // 4, SLICE_TOK + 1), jax.random.fold_in(seeds[9], 1), SLICE_TOK // 4, SLICE_TOK).astype(jnp.int32)
    return {"forward_input": forward_input, "stored_input": stored_input, "output_cotangent": output_cotangent, "norm_gain": norm_gain, "query_weight": query_weight, "key_weight": key_weight, "value_weight": value_weight, "output_weight": output_weight, "frame_index": frame_index, "valid_counts": valid_counts}


NORM_EPSILON = 1e-05
MASKED_SCORE = -1e+30

def normalize(inputs, norm_scale):
    widened = inputs.astype(jnp.float32)
    inverse = lax.rsqrt(lax.optimization_barrier(jnp.mean(widened * widened, axis=-1, keepdims=True)) + NORM_EPSILON)
    return ((widened * inverse * norm_scale).astype(jnp.bfloat16), inverse)

def project(normed, weight):
    return jnp.dot(normed, weight, preferred_element_type=jnp.float32).astype(jnp.bfloat16)

def visibility(frame_index, valid_counts):
    inside = jnp.arange(SLICE_TOK, dtype=jnp.int32)
    valid_flags = (inside[None, :] < valid_counts[:, None]).reshape(TOKENS)
    return valid_flags[None, :] & (frame_index[None, :] <= frame_index[:, None])

def heads_first(matrix, head_count):
    return matrix.reshape(TOKENS, head_count, HEAD_DIM).transpose(1, 0, 2)

def shared_heads(matrix):
    return jnp.repeat(heads_first(matrix, KV_HEADS), HEADS // KV_HEADS, axis=0)

def head_forward(visible, operands):
    query_head, key_head, value_head = operands
    score_scale = 1.0 / math.sqrt(HEAD_DIM)
    scores = jnp.dot(query_head, key_head.T, preferred_element_type=jnp.float32) * score_scale
    scores = jnp.where(visible, scores, MASKED_SCORE)
    row_max = lax.optimization_barrier(jnp.max(scores, axis=1, keepdims=True))
    weights = jnp.where(visible, jnp.exp(scores - row_max), 0.0)
    row_sum = lax.optimization_barrier(jnp.sum(weights, axis=1, keepdims=True))
    attended = jnp.dot(weights.astype(jnp.bfloat16), value_head, preferred_element_type=jnp.float32) / row_sum
    return (attended.astype(jnp.bfloat16), (row_max + jnp.log(row_sum))[:, 0])

def head_backward(visible, operands):
    query_head, key_head, value_head, dout_head, log_sum, delta = operands
    score_scale = 1.0 / math.sqrt(HEAD_DIM)
    scores = jnp.dot(query_head, key_head.T, preferred_element_type=jnp.float32) * score_scale
    scores = jnp.where(visible, scores, MASKED_SCORE)
    probability = jnp.where(visible, jnp.exp(scores - log_sum[:, None]), 0.0)
    prob_grads = jnp.dot(dout_head, value_head.T, preferred_element_type=jnp.float32)
    score_grads = (probability * (prob_grads - delta[:, None])).astype(jnp.bfloat16)
    query_grad = jnp.dot(score_grads, key_head, preferred_element_type=jnp.float32) * score_scale
    key_grad = jnp.dot(score_grads.T, query_head, preferred_element_type=jnp.float32) * score_scale
    value_grad = jnp.dot(probability.astype(jnp.bfloat16).T, dout_head, preferred_element_type=jnp.float32)
    return (query_grad.astype(jnp.bfloat16), key_grad, value_grad)

def forward_layer(inputs, norm_scale, query_proj, key_proj, value_proj, out_proj, visible):
    normed, inverse = normalize(inputs, norm_scale)
    queries = project(normed, query_proj)
    keys = project(normed, key_proj)
    values = project(normed, value_proj)
    heads_out, log_sums = lax.map(partial(head_forward, visible), (heads_first(queries, HEADS), shared_heads(keys), shared_heads(values)))
    attended = heads_out.transpose(1, 0, 2).reshape(TOKENS, HEADS * HEAD_DIM)
    layer_out = inputs.astype(jnp.float32) + jnp.dot(attended, out_proj, preferred_element_type=jnp.float32)
    return (layer_out.astype(jnp.bfloat16), inverse, queries, keys, values, attended, log_sums)

def backward_layer(inputs, cotangent, norm_scale, query_proj, key_proj, value_proj, out_proj, visible):
    _, inverse, queries, keys, values, attended, log_sums = forward_layer(inputs, norm_scale, query_proj, key_proj, value_proj, out_proj, visible)
    dout = jnp.dot(cotangent, out_proj.T, preferred_element_type=jnp.float32).astype(jnp.bfloat16)
    deltas = lax.optimization_barrier(jnp.sum((dout.astype(jnp.float32) * attended.astype(jnp.float32)).reshape(TOKENS, HEADS, HEAD_DIM), axis=-1)).T
    query_grad, key_grad, value_grad = lax.map(partial(head_backward, visible), (heads_first(queries, HEADS), shared_heads(keys), shared_heads(values), heads_first(dout, HEADS), log_sums, deltas))
    group_size = HEADS // KV_HEADS
    query_grad = query_grad.transpose(1, 0, 2).reshape(TOKENS, HEADS * HEAD_DIM)
    key_grad = key_grad.reshape(KV_HEADS, group_size, TOKENS, HEAD_DIM).sum(axis=1).transpose(1, 0, 2).reshape(TOKENS, KV_HEADS * HEAD_DIM).astype(jnp.bfloat16)
    value_grad = value_grad.reshape(KV_HEADS, group_size, TOKENS, HEAD_DIM).sum(axis=1).transpose(1, 0, 2).reshape(TOKENS, KV_HEADS * HEAD_DIM).astype(jnp.bfloat16)
    normed_grad = jnp.dot(query_grad, query_proj.T, preferred_element_type=jnp.float32)
    normed_grad = normed_grad + jnp.dot(key_grad, key_proj.T, preferred_element_type=jnp.float32)
    normed_grad = normed_grad + jnp.dot(value_grad, value_proj.T, preferred_element_type=jnp.float32)
    scaled_grad = normed_grad * norm_scale
    widened = inputs.astype(jnp.float32)
    input_grad = cotangent.astype(jnp.float32) + inverse * scaled_grad - widened * inverse ** 3 * lax.optimization_barrier(jnp.mean(widened * scaled_grad, axis=-1, keepdims=True))
    return input_grad.astype(jnp.bfloat16)

def reference(forward_input, stored_input, output_cotangent, norm_gain, query_weight, key_weight, value_weight, output_weight, frame_index, valid_counts):
    visible = visibility(frame_index, valid_counts)

    def one_section(operands):
        fwd_inputs, bwd_inputs, cotangent, norm_scale, query_proj, key_proj, value_proj, out_proj = operands
        layer_out = forward_layer(fwd_inputs, norm_scale, query_proj, key_proj, value_proj, out_proj, visible)[0]
        input_grad = backward_layer(bwd_inputs, cotangent, norm_scale, query_proj, key_proj, value_proj, out_proj, visible)
        return (layer_out, input_grad)
    layer_out, input_grad = lax.map(one_section, (forward_input, stored_input, output_cotangent, norm_gain, query_weight, key_weight, value_weight, output_weight))
    return (jnp.roll(layer_out, 1, axis=0), jnp.roll(input_grad, -1, axis=0))
```

```python
import functools
import math

import jax
import jax.numpy as jnp
from jax import lax
from jax.experimental import pallas as pl
from jax.experimental.pallas import tpu as pltpu
from jax.sharding import PartitionSpec as P

F32 = jnp.float32
BF16 = jnp.bfloat16
D = 1024
HEAD_DIM = 64
ROWS = 128
CHIP = 256
QROWS = 1024
KB = 512
NORM_EPSILON = 1e-05
MASKED = -1e30
FIRST_MAX = -1e20
NN = (((1,), (0,)), ((), ()))
NT = (((1,), (1,)), ((), ()))

OFFSET_X = (0, 1, 3, 2)
FORWARD_ORDER = ((0, 0), (0, 1), (1, 0), (2, 0), (1, 1), (2, 1), (3, 0), (3, 1))
BACKWARD_ORDER = ((3, 0), (3, 1), (1, 1), (2, 0), (1, 0), (2, 1), (0, 0), (0, 1))
MESSAGES = 40


def dot(a, b, dims):
    return lax.dot_general(a, b, dims, preferred_element_type=F32)


def fused(
    x_f, x_b, cot_in, gain, wq_in, wk_in, wv_in, wo_in, frames, counts,
    out_f, out_b,
    xf, xb, cot, wq, wkv, wo, nb,
    kvst_b, kvst_f, kvb, kvf, aux,
    qst_b, qst_f, dost, qxb, qxf, dox,
    ws_b, ws_f, wd, wkq, wvo,
    pa, pb, sa, sb, ta, tb, ua, ub,
    acc, accq, mrow, frow,
    dkv, d0, rxh, rxf, ryh, ryf, dfst, dfin,
    ost, att, dqst, dqx, stage_f, stage_b,
    load_sem, send_sem, recv_sem,
):
    sec = lax.axis_index("section")
    seq = lax.axis_index("seq")
    n_sec = lax.axis_size("section")
    x, yh, core = seq // 8, (seq // 2) % 4, seq % 2
    other = 1 - core

    def at(xx, yy, cc):
        return {"seq": (xx * 4 + yy) * 2 + cc}

    partner = at(x, yh, other)
    xp, xm = at((x + 1) % 4, yh, core), at((x + 3) % 4, yh, core)
    yp, ym = at(x, (yh + 1) % 4, core), at(x, (yh + 3) % 4, core)
    sp, sm = {"section": (sec + 1) % n_sec}, {"section": (sec + n_sec - 1) % n_sec}

    loads = []
    for i, (src, dst) in enumerate((
        (x_b, xb), (wk_in, wkv.at[:, 0:128]), (wv_in, wkv.at[:, 128:256]),
        (wq_in, wq), (cot_in, cot), (wo_in, wo), (x_f, xf),
    )):
        copy = pltpu.make_async_copy(src, dst, load_sem.at[i])
        copy.start()
        loads.append(copy)

    barrier = pltpu.get_barrier_semaphore()
    for dev in (partner, xp, xm, yp, ym, sp, sm):
        pl.semaphore_signal(barrier, inc=1, device_id=dev, device_id_type=pl.DeviceIdType.MESH)

    used = []

    def message(src, dst, dev):
        i = len(used)
        copy = pltpu.make_async_remote_copy(
            src_ref=src, dst_ref=dst, send_sem=send_sem.at[i], recv_sem=recv_sem.at[i],
            device_id=dev, device_id_type=pl.DeviceIdType.MESH,
        )
        used.append(copy)
        return copy

    mine = pl.ds(pl.multiple_of(core * ROWS, ROWS), ROWS)

    m_kvb = message(kvst_b.at[other], kvb.at[0, 0, mine], partner)
    m_kvf = message(kvst_f.at[other], kvf.at[0, 0, mine], partner)
    m_qb = message(qst_b.at[other], qxb.at[mine], partner)
    m_qf = message(qst_f.at[other], qxf.at[mine], partner)
    m_do = message(dost.at[other], dox.at[mine], partner)
    m_att = message(ost.at[other], att.at[core], partner)
    m_dq = message(dqst.at[other], dqx.at[core], partner)
    m_dkv = message(dfst.at[other], dfin.at[core], partner)

    class Gather:
        def __init__(self, kv):
            self.y = (message(kv.at[0, 0], kv.at[0, 3], yp), message(kv.at[0, 0], kv.at[0, 1], ym))
            self.y2 = (
                message(kv.at[0, 3, 0:128], kv.at[0, 2, 0:128], yp),
                message(kv.at[0, 1, 128:256], kv.at[0, 2, 128:256], ym),
            )
            self.x = tuple(
                (
                    message(kv.at[0, 2 * h:2 * h + 2], kv.at[2, 2 * h:2 * h + 2], xp),
                    message(kv.at[0, 2 * h:2 * h + 2], kv.at[1, 2 * h:2 * h + 2], xm),
                )
                for h in range(2)
            )
            self.x2 = (
                message(kv.at[2, 0:2], kv.at[3, 0:2], xp),
                message(kv.at[1, 2:4], kv.at[3, 2:4], xm),
            )

        def start(self):
            self.y[0].start()
            self.y[1].start()

        def step1(self):
            self.y[0].wait_recv()
            self.y[1].wait_recv()
            self.y2[0].start()
            self.y2[1].start()
            self.x[0][0].start()
            self.x[0][1].start()

        def step2(self):
            self.y2[0].wait_recv()
            self.y2[1].wait_recv()
            self.x[1][0].start()
            self.x[1][1].start()

        def step3(self):
            self.x[0][0].wait_recv()
            self.x2[0].start()
            self.x[0][1].wait_recv()

        def step4(self):
            self.x[1][1].wait_recv()
            self.x2[1].start()
            self.x[1][0].wait_recv()

    gather_b, gather_f = Gather(kvb), Gather(kvf)

    r_half = (message(dkv.at[3, 0:2], rxh.at[0], xp), message(dkv.at[3, 2:4], rxh.at[1], xm))
    r_full = {
        (1, h): message(dkv.at[1, 2 * h:2 * h + 2], rxf.at[0, h], xp) for h in range(2)
    } | {
        (2, h): message(dkv.at[2, 2 * h:2 * h + 2], rxf.at[1, h], xm) for h in range(2)
    }
    ry_half = (
        message(dkv.at[0, 2, 0:128], ryh.at[0], yp), message(dkv.at[0, 2, 128:256], ryh.at[1], ym),
    )
    ry_full = (message(dkv.at[0, 1], ryf.at[0], yp), message(dkv.at[0, 3], ryf.at[1], ym))

    m_out_f = message(stage_f, out_f, sp)
    m_out_b = message(stage_b, out_b, sm)
    assert len(used) == MESSAGES

    def normalize(inputs):
        wide = inputs[...].astype(F32)
        inverse = lax.rsqrt(jnp.mean(wide * wide, axis=-1, keepdims=True) + NORM_EPSILON)
        return (wide * inverse * gain[...]).astype(BF16), inverse

    def key_values(normed, staged, kv):
        both = dot(normed, wkv[...], NN)
        staged[0] = jnp.concatenate([both[:, 0:64], both[:, 128:192]], axis=1).astype(BF16)
        staged[1] = jnp.concatenate([both[:, 64:128], both[:, 192:256]], axis=1).astype(BF16)
        kv[0, 0, mine] = staged[core]

    def halves(value, staged, whole):
        staged[0] = value[:, 0:256].astype(BF16)
        staged[1] = value[:, 256:512].astype(BF16)
        whole[mine] = staged[core]

    loads[0].wait()
    normed_b, inverse_b = normalize(xb)
    nb[...] = normed_b
    loads[1].wait()
    loads[2].wait()
    key_values(nb[...], kvst_b, kvb)
    pl.semaphore_wait(barrier, 7)
    m_kvb.start()
    loads[3].wait()
    halves(dot(nb[...], wq[...], NN) * 0.125, qst_b, qxb)
    m_qb.start()
    m_kvb.wait_recv()
    gather_b.start()
    loads[4].wait()
    loads[5].wait()
    halves(dot(cot[...], wo[...], NT), dost, dox)
    m_do.start()
    gather_b.step1()

    loads[6].wait()
    normed_f, _ = normalize(xf)
    nb[...] = normed_f
    key_values(nb[...], kvst_f, kvf)
    m_kvf.start()

    chip = x * 4 + yh

    def mask_block(k, carry):
        pos, dy = k // 4, k % 4
        dx = jnp.where(pos == 2, 3, jnp.where(pos == 3, 2, pos))
        chip_k = ((x + dx) % 4) * 4 + (yh + dy) % 4
        number = lax.broadcasted_iota(jnp.int32, (128, 128), 0)
        lane = lax.broadcasted_iota(jnp.int32, (128, 128), 1)
        for h in range(2):
            row = frames[pl.ds(2 * chip_k + h, 1), :]
            seen = (row <= number) & (lane < counts[2 * chip_k + h])
            bias = jnp.where(seen | (number >= 16), 0.0, MASKED)
            aux[pos, dy, h * 128:(h + 1) * 128, :] = bias.T.astype(BF16)
        return carry

    lax.fori_loop(0, 16, mask_block, 0)

    number = lax.broadcasted_iota(jnp.int32, (128, 128), 0)
    one_hot = jnp.concatenate(
        [(frames[pl.ds(2 * chip + h, 1), :] == number).astype(F32) for h in range(2)], axis=1
    ).astype(BF16)

    def query_operand(whole, ws):
        turned = whole[...].astype(F32).T.astype(BF16)
        for h in range(4):
            cols = pl.ds(h * CHIP, CHIP)
            ws[0:64, cols] = turned[h * 64:(h + 1) * 64, :]
            ws[64:128, cols] = jnp.zeros((64, CHIP), BF16)
            ws[128:256, cols] = one_hot

    gather_b.step2()
    halves(dot(nb[...], wq[...], NN) * 0.125, qst_f, qxf)
    m_qf.start()
    m_qb.wait_recv()
    query_operand(qxb, ws_b)
    gather_b.step3()
    m_do.wait_recv()
    turned = dox[...].astype(F32).T.astype(BF16)
    nothing = jnp.zeros((CHIP, 64), F32)
    for h in range(4):
        cols = pl.ds(h * CHIP, CHIP)
        wd[0:64, cols] = jnp.zeros((64, CHIP), BF16)
        wd[64:128, cols] = turned[h * 64:(h + 1) * 64, :]
        head_q = qxb[:, h * 64:(h + 1) * 64].astype(F32)
        head_o = dox[:, h * 64:(h + 1) * 64].astype(F32)
        wkq[cols, :] = jnp.concatenate([head_q, nothing], axis=1).astype(BF16)
        wvo[cols, :] = jnp.concatenate([nothing, head_o], axis=1).astype(BF16)
    gather_b.step4()
    m_kvf.wait_recv()
    gather_f.start()
    m_qf.wait_recv()
    query_operand(qxf, ws_f)

    PS, SS = (pa, pb), (sa, sb)

    def keys_of(kv, block):
        pos, half = block
        return kv[pos, 2 * half:2 * half + 2].reshape(KB, 128)

    def attention(kv, ws, hooks):
        acc[...] = jnp.zeros_like(acc)
        maxima = []
        lane = lax.broadcasted_iota(jnp.int32, (KB, 128), 1)
        for t in range(10):
            if t in hooks:
                hooks[t]()
            if t < 8:
                operand = jnp.concatenate(
                    [keys_of(kv, FORWARD_ORDER[t]), keys_of(aux, FORWARD_ORDER[t])], axis=1
                )
                tops = []
                for r in range(4):
                    cols = pl.ds(r * CHIP, CHIP)
                    scores = dot(operand, ws[:, cols], NN)
                    SS[t % 2][:, cols] = scores
                    tops.append(jnp.max(scores.reshape(KB // 8, 8, CHIP), axis=0))
                top = jnp.max(jnp.concatenate(tops, axis=1), axis=0, keepdims=True)
                before = maxima[-1] if maxima else jnp.full((1, QROWS), FIRST_MAX, F32)
                maxima.append(jnp.maximum(before, top))
                mrow[t:t + 1, :] = maxima[-1]
            if 1 <= t <= 8:
                n = t - 1
                for r in range(4):
                    cols = pl.ds(r * CHIP, CHIP)
                    PS[n % 2][n // 2, :, cols] = jnp.exp(
                        SS[n % 2][:, cols] - maxima[n][:, r * CHIP:(r + 1) * CHIP]
                    ).astype(BF16)
            if t >= 2:
                n = t - 2
                block = keys_of(kv, FORWARD_ORDER[n])
                turned = jnp.where(lane < 64, jnp.ones_like(block), block).T
                term = dot(turned, PS[n % 2][n // 2], NN)
                if n == 0:
                    acc[...] = term
                else:
                    acc[...] = acc[...] * jnp.exp(maxima[n - 1] - maxima[n]) + term
        return maxima[-1]

    def tokens_first(columns, staged, whole):
        tall = jnp.concatenate([columns[:, h * CHIP:(h + 1) * CHIP] for h in range(4)], axis=0)
        rows = tall.T.astype(BF16)
        staged[0] = rows[0:128]
        staged[1] = rows[128:256]
        whole[core] = staged[core]

    def wait_x2():
        gather_b.x2[0].wait_recv()
        gather_b.x2[1].wait_recv()

    final_max = attention(
        kvb, ws_b, {2: gather_f.step1, 4: gather_f.step2, 6: wait_x2}
    )
    inverse_sum = 1.0 / acc[0:1, :]
    attended = (acc[64:128, :] * inverse_sum).astype(BF16).astype(F32)
    delta = jnp.sum(wd[64:128, :].astype(F32) * attended, axis=0, keepdims=True)
    frow[...] = jnp.exp(mrow[...] - final_max) * inverse_sum

    TS, US = (ta, tb), (ua, ub)
    accq[...] = jnp.zeros_like(accq)

    for t in range(9):
        if t == 1:
            gather_f.step3()
        if t == 3:
            gather_f.step4()
        if t < 8:
            n = FORWARD_ORDER.index(BACKWARD_ORDER[t])
            keys = keys_of(kvb, BACKWARD_ORDER[t])
            for r in range(4):
                cols = pl.ds(r * CHIP, CHIP)
                grads = dot(keys, wd[:, cols], NN) - delta[:, r * CHIP:(r + 1) * CHIP]
                prob = PS[n % 2][n // 2, :, cols].astype(F32) * frow[n:n + 1, cols]
                TS[t % 2][:, cols] = prob.astype(BF16)
                US[t % 2][:, cols] = (prob * grads).astype(BF16)
        if t >= 1:
            pos, half = BACKWARD_ORDER[t - 1]
            score_grads = US[(t - 1) % 2][...]
            accq[...] += dot(keys_of(kvb, (pos, half)).T, score_grads, NN)
            terms = dot(score_grads, wkq[...], NN) + dot(TS[(t - 1) % 2][...], wvo[...], NN)
            terms = terms.reshape(2, CHIP, 128)
            if (pos, half) == (1, 0):
                r_half[0].wait_recv()
                terms = terms + rxh[0].astype(F32)
            if (pos, half) == (2, 1):
                r_half[1].wait_recv()
                terms = terms + rxh[1].astype(F32)
            if pos == 0:
                d0[2 * half:2 * half + 2] = terms
            else:
                dkv[pos, 2 * half:2 * half + 2] = terms.astype(BF16)
                (r_half[half] if pos == 3 else r_full[(pos, half)]).start()

    tokens_first(accq[0:64, :] * 0.125, dqst, dqx)
    m_dq.start()

    def sum_x():
        for half in range(2):
            r_full[(1, half)].wait_recv()
            r_full[(2, half)].wait_recv()
            whole = (
                d0[2 * half:2 * half + 2] + rxf[0, half].astype(F32) + rxf[1, half].astype(F32)
            )
            d0[2 * half:2 * half + 2] = whole
        dkv[0, 2] = d0[2].astype(BF16)
        ry_half[0].start()
        ry_half[1].start()

    def sum_y():
        ry_half[0].wait_recv()
        dkv[0, 1, 0:128] = (d0[1, 0:128] + ryh[0].astype(F32)).astype(BF16)
        dkv[0, 1, 128:256] = d0[1, 128:256].astype(BF16)
        ry_full[0].start()
        ry_half[1].wait_recv()
        dkv[0, 3, 0:128] = d0[3, 0:128].astype(BF16)
        dkv[0, 3, 128:256] = (d0[3, 128:256] + ryh[1].astype(F32)).astype(BF16)
        ry_full[1].start()

    def sum_own():
        ry_full[0].wait_recv()
        ry_full[1].wait_recv()
        whole = (d0[0] + ryf[0].astype(F32) + ryf[1].astype(F32)).astype(BF16)
        dfst[0] = whole[0:128]
        dfst[1] = whole[128:256]
        dfin[core] = dfst[core]
        m_dkv.start()

    def finish_backward():
        m_dq.wait_recv()
        m_dkv.wait_recv()
        first, second = dfin[0].astype(F32), dfin[1].astype(F32)
        key_value = jnp.concatenate(
            [first[:, 0:64], second[:, 0:64], first[:, 64:128], second[:, 64:128]], axis=1
        ).astype(BF16)
        grads = dot(jnp.concatenate([dqx[0], dqx[1]], axis=1), wq[...], NT)
        grads = grads + dot(key_value, wkv[...], NT)
        scaled = grads * gain[...]
        wide = xb[...].astype(F32)
        inverse = lax.rsqrt(jnp.mean(wide * wide, axis=-1, keepdims=True) + NORM_EPSILON)
        mean = jnp.mean(wide * scaled, axis=-1, keepdims=True)
        stage_b[...] = (
            cot[...].astype(F32) + inverse * scaled - wide * (inverse * inverse * inverse) * mean
        ).astype(BF16)
        m_out_b.start()

    def wait_f():
        gather_f.x2[0].wait_recv()
        gather_f.x2[1].wait_recv()

    def hook6():
        wait_f()
        sum_own()

    attention(kvf, ws_f, {2: sum_x, 4: sum_y, 6: hook6, 8: finish_backward})
    tokens_first(acc[64:128, :] * (1.0 / acc[0:1, :]), ost, att)
    m_att.start()
    m_att.wait_recv()
    stage_f[...] = (
        xf[...].astype(F32) + dot(jnp.concatenate([att[0], att[1]], axis=1), wo[...], NN)
    ).astype(BF16)
    m_out_f.start()
    for copy in used:
        copy.wait_send()
    m_out_b.wait_recv()
    m_out_f.wait_recv()


def on_device(
    forward_input, stored_input, output_cotangent, norm_gain,
    query_weight, key_weight, value_weight, output_weight, frame_index, valid_counts,
):
    any_space = pl.BlockSpec(memory_space=pl.ANY)
    vmem = pl.BlockSpec(memory_space=pltpu.VMEM)
    shape = jax.ShapeDtypeStruct((ROWS, D), BF16)
    scratch = [
        (ROWS, D), (ROWS, D), (ROWS, D), (D, 512), (D, 256), (512, D), (ROWS, D),
        (2, ROWS, 128), (2, ROWS, 128), (4, 4, CHIP, 128), (4, 4, CHIP, 128), (4, 4, CHIP, 128),
        (2, ROWS, 256), (2, ROWS, 256), (2, ROWS, 256), (CHIP, 256), (CHIP, 256), (CHIP, 256),
        (256, QROWS), (256, QROWS), (128, QROWS), (QROWS, 128), (QROWS, 128),
        (4, KB, QROWS), (4, KB, QROWS), ((KB, QROWS), F32), ((KB, QROWS), F32),
        (KB, QROWS), (KB, QROWS), (KB, QROWS), (KB, QROWS),
        ((128, QROWS), F32), ((128, QROWS), F32), ((8, QROWS), F32), ((8, QROWS), F32),
        (4, 4, CHIP, 128), ((4, CHIP, 128), F32), (2, 2, CHIP, 128), (2, 2, 2, CHIP, 128),
        (2, ROWS, 128), (2, CHIP, 128), (2, ROWS, 128), (2, ROWS, 128),
        (2, ROWS, 256), (2, ROWS, 256), (2, ROWS, 256), (2, ROWS, 256), (ROWS, D), (ROWS, D),
    ]
    scratch = [
        pltpu.VMEM(*s) if isinstance(s[1], type) or not isinstance(s[1], int) else pltpu.VMEM(s, BF16)
        for s in scratch
    ]
    out_f, out_b = pl.pallas_call(
        fused,
        out_shape=(shape, shape),
        in_specs=[any_space] * 3 + [vmem] + [any_space] * 4
        + [vmem, pl.BlockSpec(memory_space=pltpu.SMEM)],
        out_specs=(any_space, any_space),
        scratch_shapes=scratch + [
            pltpu.SemaphoreType.DMA((7,)),
            pltpu.SemaphoreType.DMA((MESSAGES,)),
            pltpu.SemaphoreType.DMA((MESSAGES,)),
        ],
        compiler_params=pltpu.CompilerParams(
            collective_id=0, has_side_effects=True, vmem_limit_bytes=56 * 2**20
        ),
        name="sublayer",
    )(
        forward_input[0], stored_input[0], output_cotangent[0], norm_gain,
        query_weight[0], key_weight[0], value_weight[0], output_weight[0],
        frame_index.reshape(32, 128), valid_counts,
    )
    return out_f[None], out_b[None]


def solution(mesh):
    return jax.shard_map(
        on_device,
        mesh=mesh,
        in_specs=(
            P("section", "seq", None),
            P("section", "seq", None),
            P("section", "seq", None),
            P("section", None),
            P("section", None, None),
            P("section", None, None),
            P("section", None, None),
            P("section", None, None),
            P(),
            P(),
        ),
        out_specs=(P("section", "seq", None), P("section", "seq", None)),
        check_vma=False,
    )
```

```python
import jax
import jax.numpy as jnp
from jax import lax
from jax.experimental import pallas as pl
from jax.experimental.pallas import tpu as pltpu
from jax.sharding import PartitionSpec as P

F32 = jnp.float32
BF16 = jnp.bfloat16
D = 1024
HEAD_DIM = 64
ROWS = 128
CHIP = 256
QROWS = 1024
KB = 512
NORM_EPSILON = 1e-05
MASKED = -1e30
FIRST_MAX = -1e20
NN = (((1,), (0,)), ((), ()))
NT = (((1,), (1,)), ((), ()))

FORWARD_ORDER = ((0, 0), (0, 1), (1, 0), (3, 0), (2, 0), (2, 1), (1, 1), (3, 1))
BACKWARD_ORDER = ((2, 1), (2, 0), (1, 1), (1, 0), (3, 1), (3, 0), (0, 1), (0, 0))
MESSAGES = 61


def dot(a, b, dims):
    return lax.dot_general(a, b, dims, preferred_element_type=F32)


def fused(
    x_f, x_b, cot_in, gain, wq_in, wk_in, wv_in, wo_in, frames, counts,
    out_f, out_b,
    xf, xb, cot, wq, wkv, wo, nb,
    kvst_b, kvst_f, kvb, kvf, aux,
    qst_b, qst_f, dost, qxb, qxf, dox,
    ws_b, ws_f, wd, wkq, wvo,
    pa, pb, sa, sb, ta, tb, ua, ub,
    acc, accq, mrow, frow,
    dkv, d0, rx, ry, dfst, dfin, part,
    ost, att, dqst, dqx, stage_f, stage_b,
    load_sem, send_sem, recv_sem,
):
    sec = lax.axis_index("section")
    seq = lax.axis_index("seq")
    n_sec = lax.axis_size("section")
    x, yh, core = seq // 8, (seq // 2) % 4, seq % 2
    other = 1 - core

    def at(xx, yy, cc):
        return {"seq": (xx * 4 + yy) * 2 + cc}

    partner = at(x, yh, other)
    xp, xm = at((x + 1) % 4, yh, core), at((x + 3) % 4, yh, core)
    yp, ym = at(x, (yh + 1) % 4, core), at(x, (yh + 3) % 4, core)
    x2, y2 = at((x + 2) % 4, yh, core), at(x, (yh + 2) % 4, core)
    sp, sm = {"section": (sec + 1) % n_sec}, {"section": (sec + n_sec - 1) % n_sec}

    loads = []
    for i, (src, dst) in enumerate((
        (x_b, xb), (wk_in, wkv.at[:, 0:128]), (wv_in, wkv.at[:, 128:256]),
        (wq_in, wq), (cot_in, cot), (wo_in, wo), (x_f, xf),
    )):
        copy = pltpu.make_async_copy(src, dst, load_sem.at[i])
        copy.start()
        loads.append(copy)

    barrier = pltpu.get_barrier_semaphore()
    for dev in (partner, xp, xm, x2, yp, ym, y2, sp, sm):
        pl.semaphore_signal(barrier, inc=1, device_id=dev, device_id_type=pl.DeviceIdType.MESH)

    used = []

    def message(src, dst, dev):
        i = len(used)
        copy = pltpu.make_async_remote_copy(
            src_ref=src, dst_ref=dst, send_sem=send_sem.at[i], recv_sem=recv_sem.at[i],
            device_id=dev, device_id_type=pl.DeviceIdType.MESH,
        )
        used.append(copy)
        return copy

    mine = pl.ds(pl.multiple_of(core * ROWS, ROWS), ROWS)

    m_kvb = message(kvst_b.at[other], kvb.at[0, 0, mine], partner)
    m_kvf = message(kvst_f.at[other], kvf.at[0, 0, mine], partner)
    m_qb = message(qst_b.at[other], qxb.at[mine], partner)
    m_qf = message(qst_f.at[other], qxf.at[mine], partner)
    m_do = message(dost.at[other], dox.at[mine], partner)
    m_att = message(ost.at[other], att.at[core], partner)
    m_dq = message(dqst.at[other], dqx.at[core], partner)
    m_dkv = message(dfst.at[other], dfin.at[core], partner)

    class Gather:
        def __init__(self, kv):
            own = kv.at[0, 0]
            self.y = (
                message(own, kv.at[3, 0], yp), message(own, kv.at[1, 0], ym),
                message(own, kv.at[2, 0], y2),
            )
            self.x = tuple(
                (message(kv.at[d, 0], kv.at[d, 2], xp), message(kv.at[d, 0], kv.at[d, 1], xm))
                for d in range(4)
            )
            self.far = {
                d: (
                    message(kv.at[d, 2, 0:128], kv.at[d, 3, 0:128], xp),
                    message(kv.at[d, 1, 128:256], kv.at[d, 3, 128:256], xm),
                )
                for d in (0, 1, 3)
            }
            self.far[2] = (message(kv.at[2, 0], kv.at[2, 3], x2),)

        def start_y(self):
            for copy in self.y:
                copy.start()

        def start_x(self, d):
            for copy in self.x[d]:
                copy.start()

        def near(self):
            self.y[0].wait_recv()
            self.start_x(3)
            self.y[1].wait_recv()
            self.start_x(1)

        def middle(self):
            self.y[2].wait_recv()
            self.start_x(2)
            self.far[2][0].start()

        def forward(self, d):
            self.x[d][0].wait_recv()
            self.far[d][0].start()
            self.x[d][1].wait_recv()
            self.far[d][1].start()

        def wait_x(self, d):
            for copy in self.x[d]:
                copy.wait_recv()

        def wait_far(self, d):
            for copy in self.far[d]:
                copy.wait_recv()

    gather_b, gather_f = Gather(kvb), Gather(kvf)

    sum_x = {
        (d, p): message(dkv.at[d, p], rx.at[d, p - 1], dev)
        for d in range(4) for p, dev in ((1, xp), (2, xm), (3, x2))
    }
    sum_y = {d: message(dkv.at[d, 0], ry.at[d - 1], dev) for d, dev in ((1, yp), (2, y2), (3, ym))}

    m_out_f = message(stage_f, out_f, sp)
    m_out_b = message(stage_b, out_b, sm)
    assert len(used) == MESSAGES

    def normalize(inputs):
        wide = inputs[...].astype(F32)
        inverse = lax.rsqrt(jnp.mean(wide * wide, axis=-1, keepdims=True) + NORM_EPSILON)
        return (wide * inverse * gain[...]).astype(BF16), inverse

    def key_values(normed, staged, kv):
        both = dot(normed, wkv[...], NN)
        staged[0] = jnp.concatenate([both[:, 0:64], both[:, 128:192]], axis=1).astype(BF16)
        staged[1] = jnp.concatenate([both[:, 64:128], both[:, 192:256]], axis=1).astype(BF16)
        kv[0, 0, mine] = staged[core]

    def halves(value, staged, whole):
        staged[0] = value[:, 0:256].astype(BF16)
        staged[1] = value[:, 256:512].astype(BF16)
        whole[mine] = staged[core]

    loads[0].wait()
    normed_b, inverse_b = normalize(xb)
    nb[...] = normed_b
    loads[1].wait()
    loads[2].wait()
    key_values(nb[...], kvst_b, kvb)
    pl.semaphore_wait(barrier, 9)
    m_kvb.start()
    loads[3].wait()
    halves(dot(nb[...], wq[...], NN) * 0.125, qst_b, qxb)
    m_qb.start()
    m_kvb.wait_recv()
    gather_b.start_y()
    gather_b.start_x(0)
    loads[4].wait()
    loads[5].wait()
    halves(dot(cot[...], wo[...], NT), dost, dox)
    m_do.start()

    loads[6].wait()
    normed_f, _ = normalize(xf)
    nb[...] = normed_f
    key_values(nb[...], kvst_f, kvf)
    m_kvf.start()
    gather_b.forward(0)

    chip = x * 4 + yh

    def mask_block(k, carry):
        dy, pos = k // 4, k % 4
        dx = jnp.where(pos == 2, 3, jnp.where(pos == 3, 2, pos))
        chip_k = ((x + dx) % 4) * 4 + (yh + dy) % 4
        number = lax.broadcasted_iota(jnp.int32, (128, 128), 0)
        lane = lax.broadcasted_iota(jnp.int32, (128, 128), 1)
        for h in range(2):
            row = frames[pl.ds(2 * chip_k + h, 1), :]
            seen = (row <= number) & (lane < counts[2 * chip_k + h])
            bias = jnp.where(seen | (number >= 16), 0.0, MASKED)
            aux[dy, pos, h * 128:(h + 1) * 128, :] = bias.T.astype(BF16)
        return carry

    lax.fori_loop(0, 16, mask_block, 0)

    number = lax.broadcasted_iota(jnp.int32, (128, 128), 0)
    one_hot = jnp.concatenate(
        [(frames[pl.ds(2 * chip + h, 1), :] == number).astype(F32) for h in range(2)], axis=1
    ).astype(BF16)

    def query_operand(whole, ws):
        turned = whole[...].astype(F32).T.astype(BF16)
        for h in range(4):
            cols = pl.ds(h * CHIP, CHIP)
            ws[0:64, cols] = turned[h * 64:(h + 1) * 64, :]
            ws[64:128, cols] = jnp.zeros((64, CHIP), BF16)
            ws[128:256, cols] = one_hot

    gather_b.near()
    halves(dot(nb[...], wq[...], NN) * 0.125, qst_f, qxf)
    m_qf.start()
    m_qb.wait_recv()
    query_operand(qxb, ws_b)
    gather_b.middle()
    m_kvf.wait_recv()
    gather_f.start_y()
    gather_f.start_x(0)
    m_do.wait_recv()
    turned = dox[...].astype(F32).T.astype(BF16)
    nothing = jnp.zeros((CHIP, 64), F32)
    for h in range(4):
        cols = pl.ds(h * CHIP, CHIP)
        wd[0:64, cols] = jnp.zeros((64, CHIP), BF16)
        wd[64:128, cols] = turned[h * 64:(h + 1) * 64, :]
        head_q = qxb[:, h * 64:(h + 1) * 64].astype(F32)
        head_o = dox[:, h * 64:(h + 1) * 64].astype(F32)
        wkq[cols, :] = jnp.concatenate([head_q, nothing], axis=1).astype(BF16)
        wvo[cols, :] = jnp.concatenate([nothing, head_o], axis=1).astype(BF16)
    gather_b.forward(1)
    gather_b.forward(3)
    m_qf.wait_recv()
    query_operand(qxf, ws_f)

    PS, SS = (pa, pb), (sa, sb)

    def keys_of(kv, block):
        d, half = block
        return kv[d, 2 * half:2 * half + 2].reshape(KB, 128)

    def attention(kv, ws, hooks):
        acc[...] = jnp.zeros_like(acc)
        maxima = []
        lane = lax.broadcasted_iota(jnp.int32, (KB, 128), 1)
        for t in range(10):
            if t in hooks:
                hooks[t]()
            if t < 8:
                operand = jnp.concatenate(
                    [keys_of(kv, FORWARD_ORDER[t]), keys_of(aux, FORWARD_ORDER[t])], axis=1
                )
                tops = []
                for r in range(4):
                    cols = pl.ds(r * CHIP, CHIP)
                    scores = dot(operand, ws[:, cols], NN)
                    SS[t % 2][:, cols] = scores
                    tops.append(jnp.max(scores.reshape(KB // 8, 8, CHIP), axis=0))
                top = jnp.max(jnp.concatenate(tops, axis=1), axis=0, keepdims=True)
                before = maxima[-1] if maxima else jnp.full((1, QROWS), FIRST_MAX, F32)
                maxima.append(jnp.maximum(before, top))
                mrow[t:t + 1, :] = maxima[-1]
            if 1 <= t <= 8:
                n = t - 1
                for r in range(4):
                    cols = pl.ds(r * CHIP, CHIP)
                    PS[n % 2][n // 2, :, cols] = jnp.exp(
                        SS[n % 2][:, cols] - maxima[n][:, r * CHIP:(r + 1) * CHIP]
                    ).astype(BF16)
            if t >= 2:
                n = t - 2
                block = keys_of(kv, FORWARD_ORDER[n])
                turned = jnp.where(lane < 64, jnp.ones_like(block), block).T
                term = dot(turned, PS[n % 2][n // 2], NN)
                if n == 0:
                    acc[...] = term
                else:
                    acc[...] = acc[...] * jnp.exp(maxima[n - 1] - maxima[n]) + term
        return maxima[-1]

    def tokens_first(columns, staged, whole):
        tall = jnp.concatenate([columns[:, h * CHIP:(h + 1) * CHIP] for h in range(4)], axis=0)
        rows = tall.T.astype(BF16)
        staged[0] = rows[0:128]
        staged[1] = rows[128:256]
        whole[core] = staged[core]

    def last_f():
        gather_b.wait_far(1)
        gather_f.near()

    def middle_f():
        gather_b.wait_far(3)
        gather_f.middle()

    final_max = attention(
        kvb, ws_b,
        {
            1: lambda: gather_b.wait_far(0),
            2: lambda: gather_f.forward(0),
            4: lambda: gather_b.wait_x(2),
            5: lambda: gather_b.wait_far(2),
            6: last_f,
            7: middle_f,
        },
    )
    inverse_sum = 1.0 / acc[0:1, :]
    attended = (acc[64:128, :] * inverse_sum).astype(BF16).astype(F32)
    delta = jnp.sum(wd[64:128, :].astype(F32) * attended, axis=0, keepdims=True)
    frow[...] = jnp.exp(mrow[...] - final_max) * inverse_sum

    def add_x(d):
        whole = d0[d]
        for p in (1, 2, 3):
            sum_x[(d, p)].wait_recv()
            whole = whole + rx[d, p - 1].astype(F32)
        dkv[d, 0] = whole.astype(BF16)
        sum_y[d].start()

    TS, US = (ta, tb), (ua, ub)
    accq[...] = jnp.zeros_like(accq)

    for t in range(9):
        if t == 3:
            gather_f.forward(1)
        if t == 4:
            gather_f.forward(3)
        if t == 8:
            gather_f.wait_x(2)
            add_x(2)
        if t < 8:
            n = FORWARD_ORDER.index(BACKWARD_ORDER[t])
            keys = keys_of(kvb, BACKWARD_ORDER[t])
            for r in range(4):
                cols = pl.ds(r * CHIP, CHIP)
                grads = dot(keys, wd[:, cols], NN) - delta[:, r * CHIP:(r + 1) * CHIP]
                prob = PS[n % 2][n // 2, :, cols].astype(F32) * frow[n:n + 1, cols]
                TS[t % 2][:, cols] = prob.astype(BF16)
                US[t % 2][:, cols] = (prob * grads).astype(BF16)
        if t >= 1:
            d, half = BACKWARD_ORDER[t - 1]
            score_grads = US[(t - 1) % 2][...]
            accq[...] += dot(keys_of(kvb, (d, half)).T, score_grads, NN)
            terms = dot(score_grads, wkq[...], NN) + dot(TS[(t - 1) % 2][...], wvo[...], NN)
            if half == 0:
                d0[d] = terms[0:CHIP]
                dkv[d, 1] = terms[CHIP:].astype(BF16)
                sum_x[(d, 1)].start()
            else:
                dkv[d, 2] = terms[0:CHIP].astype(BF16)
                dkv[d, 3] = terms[CHIP:].astype(BF16)
                sum_x[(d, 3)].start()
                sum_x[(d, 2)].start()

    tokens_first(accq[0:64, :] * 0.125, dqst, dqx)
    m_dq.start()

    def query_part():
        m_dq.wait_recv()
        part[...] = dot(jnp.concatenate([dqx[0], dqx[1]], axis=1), wq[...], NT)

    def sum_own():
        whole = d0[0]
        for p in (1, 2, 3):
            sum_x[(0, p)].wait_recv()
            whole = whole + rx[0, p - 1].astype(F32)
        for d in (1, 3, 2):
            sum_y[d].wait_recv()
            whole = whole + ry[d - 1].astype(F32)
        whole = whole.astype(BF16)
        dfst[0] = whole[0:128]
        dfst[1] = whole[128:256]
        dfin[core] = dfst[core]
        m_dkv.start()

    def finish_backward():
        m_dkv.wait_recv()
        first, second = dfin[0].astype(F32), dfin[1].astype(F32)
        key_value = jnp.concatenate(
            [first[:, 0:64], second[:, 0:64], first[:, 64:128], second[:, 64:128]], axis=1
        ).astype(BF16)
        grads = part[...] + dot(key_value, wkv[...], NT)
        scaled = grads * gain[...]
        wide = xb[...].astype(F32)
        inverse = lax.rsqrt(jnp.mean(wide * wide, axis=-1, keepdims=True) + NORM_EPSILON)
        mean = jnp.mean(wide * scaled, axis=-1, keepdims=True)
        stage_b[...] = (
            cot[...].astype(F32) + inverse * scaled - wide * (inverse * inverse * inverse) * mean
        ).astype(BF16)
        m_out_b.start()

    def ready_1():
        gather_f.wait_far(1)
        add_x(3)

    attention(
        kvf, ws_f,
        {
            1: lambda: gather_f.wait_far(0),
            3: query_part,
            4: lambda: add_x(1),
            5: lambda: gather_f.wait_far(2),
            6: ready_1,
            7: lambda: gather_f.wait_far(3),
        },
    )
    tokens_first(acc[64:128, :] * (1.0 / acc[0:1, :]), ost, att)
    m_att.start()
    sum_own()
    m_att.wait_recv()
    stage_f[...] = (
        xf[...].astype(F32) + dot(jnp.concatenate([att[0], att[1]], axis=1), wo[...], NN)
    ).astype(BF16)
    m_out_f.start()
    finish_backward()
    for copy in used:
        copy.wait_send()
    m_out_b.wait_recv()
    m_out_f.wait_recv()


def hand_over(in_f, in_b, out_f, out_b, sem):
    copies = [
        pltpu.make_async_copy(in_f, out_f, sem.at[0]), pltpu.make_async_copy(in_b, out_b, sem.at[1]),
    ]
    for copy in copies:
        copy.start()
    for copy in copies:
        copy.wait()


def on_device(
    forward_input, stored_input, output_cotangent, norm_gain,
    query_weight, key_weight, value_weight, output_weight, frame_index, valid_counts,
):
    any_space = pl.BlockSpec(memory_space=pl.ANY)
    vmem = pl.BlockSpec(memory_space=pltpu.VMEM)
    shape = jax.ShapeDtypeStruct((ROWS, D), BF16)
    scratch = [
        (ROWS, D), (ROWS, D), (ROWS, D), (D, 512), (D, 256), (512, D), (ROWS, D),
        (2, ROWS, 128), (2, ROWS, 128), (4, 4, CHIP, 128), (4, 4, CHIP, 128), (4, 4, CHIP, 128),
        (2, ROWS, 256), (2, ROWS, 256), (2, ROWS, 256), (CHIP, 256), (CHIP, 256), (CHIP, 256),
        (256, QROWS), (256, QROWS), (128, QROWS), (QROWS, 128), (QROWS, 128),
        (4, KB, QROWS), (4, KB, QROWS), ((KB, QROWS), F32), ((KB, QROWS), F32),
        (KB, QROWS), (KB, QROWS), (KB, QROWS), (KB, QROWS),
        ((128, QROWS), F32), ((128, QROWS), F32), ((8, QROWS), F32), ((8, QROWS), F32),
        (4, 4, CHIP, 128), ((4, CHIP, 128), F32), (4, 3, CHIP, 128), (3, CHIP, 128),
        (2, ROWS, 128), (2, ROWS, 128), ((ROWS, D), F32),
        (2, ROWS, 256), (2, ROWS, 256), (2, ROWS, 256), (2, ROWS, 256), (ROWS, D), (ROWS, D),
    ]
    scratch = [
        pltpu.VMEM(*s) if isinstance(s[1], type) or not isinstance(s[1], int) else pltpu.VMEM(s, BF16)
        for s in scratch
    ]
    out_f, out_b = pl.pallas_call(
        fused,
        out_shape=(shape, shape),
        in_specs=[any_space] * 3 + [vmem] + [any_space] * 4
        + [vmem, pl.BlockSpec(memory_space=pltpu.SMEM)],
        out_specs=(any_space, any_space),
        scratch_shapes=scratch + [
            pltpu.SemaphoreType.DMA((7,)),
            pltpu.SemaphoreType.DMA((MESSAGES,)),
            pltpu.SemaphoreType.DMA((MESSAGES,)),
        ],
        compiler_params=pltpu.CompilerParams(
            collective_id=0, has_side_effects=True, vmem_limit_bytes=56 * 2**20
        ),
        name="sublayer",
    )(
        forward_input[0], stored_input[0], output_cotangent[0], norm_gain,
        query_weight[0], key_weight[0], value_weight[0], output_weight[0],
        frame_index.reshape(32, 128), valid_counts,
    )
    out_f, out_b = pl.pallas_call(
        hand_over,
        out_shape=(shape, shape),
        in_specs=[any_space] * 2,
        out_specs=(any_space, any_space),
        scratch_shapes=[pltpu.SemaphoreType.DMA((2,))],
        name="hand_over",
    )(out_f, out_b)
    return out_f[None], out_b[None]


def solution(mesh):
    return jax.shard_map(
        on_device,
        mesh=mesh,
        in_specs=(
            P("section", "seq", None),
            P("section", "seq", None),
            P("section", "seq", None),
            P("section", None),
            P("section", None, None),
            P("section", None, None),
            P("section", None, None),
            P("section", None, None),
            P(),
            P(),
        ),
        out_specs=(P("section", "seq", None), P("section", "seq", None)),
        check_vma=False,
    )
```

```python
import jax
import jax.numpy as jnp
from jax import lax
from jax.experimental import pallas as pl
from jax.experimental.pallas import tpu as pltpu
from jax.sharding import PartitionSpec as P

F32 = jnp.float32
BF16 = jnp.bfloat16
D = 1024
HEAD_DIM = 64
ROWS = 128
CHIP = 256
QROWS = 1024
KB = 512
NORM_EPSILON = 1e-05
MASKED = -1e30
FIRST_MAX = -1e20
NN = (((1,), (0,)), ((), ()))
NT = (((1,), (1,)), ((), ()))

FORWARD_ORDER = ((0, 0), (0, 1), (1, 0), (3, 0), (2, 0), (2, 1), (1, 1), (3, 1))
BACKWARD_ORDER = ((2, 1), (2, 0), (1, 1), (1, 0), (3, 1), (3, 0), (0, 1), (0, 0))
MESSAGES = 61


def dot(a, b, dims):
    return lax.dot_general(a, b, dims, preferred_element_type=F32)


def fused(
    x_f, x_b, cot_in, gain, wq_in, wk_in, wv_in, wo_in, frames, counts,
    out_f, out_b,
    xf, xb, cot, wq, wkv, wo, nb,
    kvst_b, kvst_f, kvb, kvf, aux,
    qst_b, qst_f, dost, qxb, qxf, dox,
    ws_b, ws_f, wd, wkq, wvo,
    pa, pb, sa, sb, ta, tb, ua, ub,
    acc, accq, mrow, frow,
    dkv, d0, rx, ry, dfst, dfin, part,
    ost, att, dqst, dqx, stage_f, stage_b,
    load_sem, send_sem, recv_sem,
):
    sec = lax.axis_index("section")
    seq = lax.axis_index("seq")
    n_sec = lax.axis_size("section")
    x, yh, core = seq // 8, (seq // 2) % 4, seq % 2
    other = 1 - core

    def at(xx, yy, cc):
        return {"seq": (xx * 4 + yy) * 2 + cc}

    partner = at(x, yh, other)
    xp, xm = at((x + 1) % 4, yh, core), at((x + 3) % 4, yh, core)
    yp, ym = at(x, (yh + 1) % 4, core), at(x, (yh + 3) % 4, core)
    x2, y2 = at((x + 2) % 4, yh, core), at(x, (yh + 2) % 4, core)
    sp, sm = {"section": (sec + 1) % n_sec}, {"section": (sec + n_sec - 1) % n_sec}

    loads = []
    for i, (src, dst) in enumerate((
        (x_b, xb), (wk_in, wkv.at[:, 0:128]), (wv_in, wkv.at[:, 128:256]),
        (wq_in, wq), (cot_in, cot), (wo_in, wo), (x_f, xf),
    )):
        copy = pltpu.make_async_copy(src, dst, load_sem.at[i])
        copy.start()
        loads.append(copy)

    barrier = pltpu.get_barrier_semaphore()
    for dev in (partner, xp, xm, x2, yp, ym, y2, sp, sm):
        pl.semaphore_signal(barrier, inc=1, device_id=dev, device_id_type=pl.DeviceIdType.MESH)

    used = []

    def message(src, dst, dev):
        i = len(used)
        copy = pltpu.make_async_remote_copy(
            src_ref=src, dst_ref=dst, send_sem=send_sem.at[i], recv_sem=recv_sem.at[i],
            device_id=dev, device_id_type=pl.DeviceIdType.MESH,
        )
        used.append(copy)
        return copy

    mine = pl.ds(pl.multiple_of(core * ROWS, ROWS), ROWS)

    m_kvb = message(kvst_b.at[other], kvb.at[0, 0, mine], partner)
    m_kvf = message(kvst_f.at[other], kvf.at[0, 0, mine], partner)
    m_qb = message(qst_b.at[other], qxb.at[mine], partner)
    m_qf = message(qst_f.at[other], qxf.at[mine], partner)
    m_do = message(dost.at[other], dox.at[mine], partner)
    m_att = message(ost.at[other], att.at[core], partner)
    m_dq = message(dqst.at[other], dqx.at[core], partner)
    m_dkv = message(dfst.at[other], dfin.at[core], partner)

    class Gather:
        def __init__(self, kv):
            own = kv.at[0, 0]
            self.y = (
                message(own, kv.at[3, 0], yp), message(own, kv.at[1, 0], ym),
                message(own, kv.at[2, 0], y2),
            )
            self.x = tuple(
                (message(kv.at[d, 0], kv.at[d, 2], xp), message(kv.at[d, 0], kv.at[d, 1], xm))
                for d in range(4)
            )
            self.far = {
                d: (
                    message(kv.at[d, 2, 0:128], kv.at[d, 3, 0:128], xp),
                    message(kv.at[d, 1, 128:256], kv.at[d, 3, 128:256], xm),
                )
                for d in (0, 1, 3)
            }
            self.far[2] = (message(kv.at[2, 0], kv.at[2, 3], x2),)

        def start_y(self):
            for copy in self.y:
                copy.start()

        def start_x(self, d):
            for copy in self.x[d]:
                copy.start()

        def near(self):
            self.y[0].wait_recv()
            self.start_x(3)
            self.y[1].wait_recv()
            self.start_x(1)

        def middle(self):
            self.y[2].wait_recv()
            self.start_x(2)
            self.far[2][0].start()

        def forward(self, d):
            self.x[d][0].wait_recv()
            self.far[d][0].start()
            self.x[d][1].wait_recv()
            self.far[d][1].start()

        def wait_x(self, d):
            for copy in self.x[d]:
                copy.wait_recv()

        def wait_far(self, d):
            for copy in self.far[d]:
                copy.wait_recv()

    gather_b, gather_f = Gather(kvb), Gather(kvf)

    sum_x = {
        (d, p): message(dkv.at[d, p], rx.at[d, p - 1], dev)
        for d in range(4) for p, dev in ((1, xp), (2, xm), (3, x2))
    }
    sum_y = {d: message(dkv.at[d, 0], ry.at[d - 1], dev) for d, dev in ((1, yp), (2, y2), (3, ym))}

    m_out_f = message(stage_f, out_f, sp)
    m_out_b = message(stage_b, out_b, sm)
    assert len(used) == MESSAGES

    def normalize(inputs):
        wide = inputs[...].astype(F32)
        inverse = lax.rsqrt(jnp.mean(wide * wide, axis=-1, keepdims=True) + NORM_EPSILON)
        return (wide * inverse * gain[...]).astype(BF16), inverse

    def key_values(normed, staged, kv):
        both = dot(normed, wkv[...], NN)
        staged[0] = jnp.concatenate([both[:, 0:64], both[:, 128:192]], axis=1).astype(BF16)
        staged[1] = jnp.concatenate([both[:, 64:128], both[:, 192:256]], axis=1).astype(BF16)
        kv[0, 0, mine] = staged[core]

    def halves(value, staged, whole):
        staged[0] = value[:, 0:256].astype(BF16)
        staged[1] = value[:, 256:512].astype(BF16)
        whole[mine] = staged[core]

    loads[0].wait()
    normed_b, inverse_b = normalize(xb)
    nb[...] = normed_b
    loads[1].wait()
    loads[2].wait()
    key_values(nb[...], kvst_b, kvb)
    pl.semaphore_wait(barrier, 9)
    m_kvb.start()
    loads[3].wait()
    halves(dot(nb[...], wq[...], NN) * 0.125, qst_b, qxb)
    m_qb.start()
    m_kvb.wait_recv()
    gather_b.start_y()
    gather_b.start_x(0)

    loads[6].wait()
    normed_f, _ = normalize(xf)
    nb[...] = normed_f
    key_values(nb[...], kvst_f, kvf)
    m_kvf.start()
    loads[4].wait()
    loads[5].wait()
    halves(dot(cot[...], wo[...], NT), dost, dox)
    m_do.start()

    chip = x * 4 + yh

    def mask_block(k, carry):
        dy, pos = k // 4, k % 4
        dx = jnp.where(pos == 2, 3, jnp.where(pos == 3, 2, pos))
        chip_k = ((x + dx) % 4) * 4 + (yh + dy) % 4
        number = lax.broadcasted_iota(jnp.int32, (128, 128), 0)
        lane = lax.broadcasted_iota(jnp.int32, (128, 128), 1)
        for h in range(2):
            row = frames[pl.ds(2 * chip_k + h, 1), :]
            seen = (row <= number) & (lane < counts[2 * chip_k + h])
            bias = jnp.where(seen | (number >= 16), 0.0, MASKED)
            aux[dy, pos, h * 128:(h + 1) * 128, :] = bias.T.astype(BF16)
        return carry

    lax.fori_loop(0, 16, mask_block, 0)

    number = lax.broadcasted_iota(jnp.int32, (128, 128), 0)
    one_hot = jnp.concatenate(
        [(frames[pl.ds(2 * chip + h, 1), :] == number).astype(F32) for h in range(2)], axis=1
    ).astype(BF16)

    def query_operand(whole, ws):
        turned = whole[...].astype(F32).T.astype(BF16)
        for h in range(4):
            cols = pl.ds(h * CHIP, CHIP)
            ws[0:64, cols] = turned[h * 64:(h + 1) * 64, :]
            ws[64:128, cols] = jnp.zeros((64, CHIP), BF16)
            ws[128:256, cols] = one_hot

    m_qb.wait_recv()
    query_operand(qxb, ws_b)
    gather_b.forward(0)
    m_kvf.wait_recv()
    gather_f.start_x(0)
    halves(dot(nb[...], wq[...], NN) * 0.125, qst_f, qxf)
    m_qf.start()
    gather_b.near()
    gather_f.start_y()
    m_do.wait_recv()
    turned = dox[...].astype(F32).T.astype(BF16)
    nothing = jnp.zeros((CHIP, 64), F32)
    for h in range(4):
        cols = pl.ds(h * CHIP, CHIP)
        wd[0:64, cols] = jnp.zeros((64, CHIP), BF16)
        wd[64:128, cols] = turned[h * 64:(h + 1) * 64, :]
        head_q = qxb[:, h * 64:(h + 1) * 64].astype(F32)
        head_o = dox[:, h * 64:(h + 1) * 64].astype(F32)
        wkq[cols, :] = jnp.concatenate([head_q, nothing], axis=1).astype(BF16)
        wvo[cols, :] = jnp.concatenate([nothing, head_o], axis=1).astype(BF16)
    m_qf.wait_recv()
    query_operand(qxf, ws_f)

    PS, SS = (pa, pb), (sa, sb)

    def keys_of(kv, block):
        d, half = block
        return kv[d, 2 * half:2 * half + 2].reshape(KB, 128)

    def attention(kv, ws, hooks):
        acc[...] = jnp.zeros_like(acc)
        maxima = []
        lane = lax.broadcasted_iota(jnp.int32, (KB, 128), 1)
        for t in range(10):
            if t in hooks:
                hooks[t]()
            if t < 8:
                operand = jnp.concatenate(
                    [keys_of(kv, FORWARD_ORDER[t]), keys_of(aux, FORWARD_ORDER[t])], axis=1
                )
                tops = []
                for r in range(4):
                    cols = pl.ds(r * CHIP, CHIP)
                    scores = dot(operand, ws[:, cols], NN)
                    SS[t % 2][:, cols] = scores
                    tops.append(jnp.max(scores.reshape(KB // 8, 8, CHIP), axis=0))
                top = jnp.max(jnp.concatenate(tops, axis=1), axis=0, keepdims=True)
                before = maxima[-1] if maxima else jnp.full((1, QROWS), FIRST_MAX, F32)
                maxima.append(jnp.maximum(before, top))
                mrow[t:t + 1, :] = maxima[-1]
            if 1 <= t <= 8:
                n = t - 1
                for r in range(4):
                    cols = pl.ds(r * CHIP, CHIP)
                    PS[n % 2][n // 2, :, cols] = jnp.exp(
                        SS[n % 2][:, cols] - maxima[n][:, r * CHIP:(r + 1) * CHIP]
                    ).astype(BF16)
            if t >= 2:
                n = t - 2
                block = keys_of(kv, FORWARD_ORDER[n])
                turned = jnp.where(lane < 64, jnp.ones_like(block), block).T
                term = dot(turned, PS[n % 2][n // 2], NN)
                if n == 0:
                    acc[...] = term
                else:
                    acc[...] = acc[...] * jnp.exp(maxima[n - 1] - maxima[n]) + term
        return maxima[-1]

    def tokens_first(columns, staged, whole):
        tall = jnp.concatenate([columns[:, h * CHIP:(h + 1) * CHIP] for h in range(4)], axis=0)
        rows = tall.T.astype(BF16)
        staged[0] = rows[0:128]
        staged[1] = rows[128:256]
        whole[core] = staged[core]

    def second_row():
        gather_b.middle()
        gather_b.forward(1)
        gather_f.forward(0)

    def last_b():
        gather_b.wait_far(1)
        gather_f.near()

    final_max = attention(
        kvb, ws_b,
        {
            1: lambda: gather_b.wait_far(0),
            2: second_row,
            3: lambda: gather_b.forward(3),
            4: lambda: gather_b.wait_x(2),
            5: lambda: gather_b.wait_far(2),
            6: last_b,
            7: lambda: gather_b.wait_far(3),
            8: gather_f.middle,
        },
    )
    inverse_sum = 1.0 / acc[0:1, :]
    attended = (acc[64:128, :] * inverse_sum).astype(BF16).astype(F32)
    delta = jnp.sum(wd[64:128, :].astype(F32) * attended, axis=0, keepdims=True)
    frow[...] = jnp.exp(mrow[...] - final_max) * inverse_sum

    def add_x(d):
        whole = d0[d]
        for p in (1, 2, 3):
            sum_x[(d, p)].wait_recv()
            whole = whole + rx[d, p - 1].astype(F32)
        dkv[d, 0] = whole.astype(BF16)
        sum_y[d].start()

    TS, US = (ta, tb), (ua, ub)
    accq[...] = jnp.zeros_like(accq)

    for t in range(9):
        if t == 4:
            gather_f.forward(1)
        if t == 5:
            gather_f.forward(3)
        if t == 8:
            add_x(2)
        if t < 8:
            n = FORWARD_ORDER.index(BACKWARD_ORDER[t])
            keys = keys_of(kvb, BACKWARD_ORDER[t])
            for r in range(4):
                cols = pl.ds(r * CHIP, CHIP)
                grads = dot(keys, wd[:, cols], NN) - delta[:, r * CHIP:(r + 1) * CHIP]
                prob = PS[n % 2][n // 2, :, cols].astype(F32) * frow[n:n + 1, cols]
                TS[t % 2][:, cols] = prob.astype(BF16)
                US[t % 2][:, cols] = (prob * grads).astype(BF16)
        if t >= 1:
            d, half = BACKWARD_ORDER[t - 1]
            score_grads = US[(t - 1) % 2][...]
            accq[...] += dot(keys_of(kvb, (d, half)).T, score_grads, NN)
            terms = dot(score_grads, wkq[...], NN) + dot(TS[(t - 1) % 2][...], wvo[...], NN)
            if half == 0:
                d0[d] = terms[0:CHIP]
                dkv[d, 1] = terms[CHIP:].astype(BF16)
                sum_x[(d, 1)].start()
            else:
                dkv[d, 2] = terms[0:CHIP].astype(BF16)
                dkv[d, 3] = terms[CHIP:].astype(BF16)
                sum_x[(d, 3)].start()
                sum_x[(d, 2)].start()

    tokens_first(accq[0:64, :] * 0.125, dqst, dqx)
    m_dq.start()

    def query_part():
        m_dq.wait_recv()
        part[...] = dot(jnp.concatenate([dqx[0], dqx[1]], axis=1), wq[...], NT)

    def add_own_x():
        whole = d0[0]
        for p in (1, 2, 3):
            sum_x[(0, p)].wait_recv()
            whole = whole + rx[0, p - 1].astype(F32)
        d0[0] = whole

    def sum_own():
        whole = d0[0]
        for d in (1, 3, 2):
            sum_y[d].wait_recv()
            whole = whole + ry[d - 1].astype(F32)
        whole = whole.astype(BF16)
        dfst[0] = whole[0:128]
        dfst[1] = whole[128:256]
        dfin[core] = dfst[core]
        m_dkv.start()

    def finish_backward():
        m_dkv.wait_recv()
        first, second = dfin[0].astype(F32), dfin[1].astype(F32)
        key_value = jnp.concatenate(
            [first[:, 0:64], second[:, 0:64], first[:, 64:128], second[:, 64:128]], axis=1
        ).astype(BF16)
        grads = part[...] + dot(key_value, wkv[...], NT)
        scaled = grads * gain[...]
        wide = xb[...].astype(F32)
        inverse = lax.rsqrt(jnp.mean(wide * wide, axis=-1, keepdims=True) + NORM_EPSILON)
        mean = jnp.mean(wide * scaled, axis=-1, keepdims=True)
        stage_b[...] = (
            cot[...].astype(F32) + inverse * scaled - wide * (inverse * inverse * inverse) * mean
        ).astype(BF16)
        m_out_b.start()

    def fourth():
        gather_f.wait_x(2)
        add_x(3)

    attention(
        kvf, ws_f,
        {
            1: lambda: (gather_f.wait_far(0), add_x(1)),
            3: query_part,
            4: fourth,
            5: lambda: gather_f.wait_far(2),
            6: lambda: gather_f.wait_far(1),
            7: lambda: gather_f.wait_far(3),
            9: add_own_x,
        },
    )
    tokens_first(acc[64:128, :] * (1.0 / acc[0:1, :]), ost, att)
    m_att.start()
    m_att.wait_recv()
    stage_f[...] = (
        xf[...].astype(F32) + dot(jnp.concatenate([att[0], att[1]], axis=1), wo[...], NN)
    ).astype(BF16)
    m_out_f.start()
    sum_own()
    finish_backward()
    for copy in used:
        copy.wait_send()
    m_out_b.wait_recv()
    m_out_f.wait_recv()


def hand_over(in_f, in_b, out_f, out_b, held, in_sem, out_sem):
    pieces = []
    for i, (src, dst) in enumerate(((in_f, out_f), (in_b, out_b))):
        for h in range(2):
            rows = pl.ds(64 * h, 64)
            arrive = pltpu.make_async_copy(src.at[rows], held.at[i, rows], in_sem.at[2 * i + h])
            leave = pltpu.make_async_copy(held.at[i, rows], dst.at[rows], out_sem.at[2 * i + h])
            arrive.start()
            pieces.append((arrive, leave))
    for arrive, leave in pieces:
        arrive.wait()
        leave.start()
    for _, leave in pieces:
        leave.wait()


def on_device(
    forward_input, stored_input, output_cotangent, norm_gain,
    query_weight, key_weight, value_weight, output_weight, frame_index, valid_counts,
):
    any_space = pl.BlockSpec(memory_space=pl.ANY)
    vmem = pl.BlockSpec(memory_space=pltpu.VMEM)
    shape = jax.ShapeDtypeStruct((ROWS, D), BF16)
    scratch = [
        (ROWS, D), (ROWS, D), (ROWS, D), (D, 512), (D, 256), (512, D), (ROWS, D),
        (2, ROWS, 128), (2, ROWS, 128), (4, 4, CHIP, 128), (4, 4, CHIP, 128), (4, 4, CHIP, 128),
        (2, ROWS, 256), (2, ROWS, 256), (2, ROWS, 256), (CHIP, 256), (CHIP, 256), (CHIP, 256),
        (256, QROWS), (256, QROWS), (128, QROWS), (QROWS, 128), (QROWS, 128),
        (4, KB, QROWS), (4, KB, QROWS), ((KB, QROWS), F32), ((KB, QROWS), F32),
        (KB, QROWS), (KB, QROWS), (KB, QROWS), (KB, QROWS),
        ((128, QROWS), F32), ((128, QROWS), F32), ((8, QROWS), F32), ((8, QROWS), F32),
        (4, 4, CHIP, 128), ((4, CHIP, 128), F32), (4, 3, CHIP, 128), (3, CHIP, 128),
        (2, ROWS, 128), (2, ROWS, 128), ((ROWS, D), F32),
        (2, ROWS, 256), (2, ROWS, 256), (2, ROWS, 256), (2, ROWS, 256), (ROWS, D), (ROWS, D),
    ]
    scratch = [
        pltpu.VMEM(*s) if isinstance(s[1], type) or not isinstance(s[1], int) else pltpu.VMEM(s, BF16)
        for s in scratch
    ]
    out_f, out_b = pl.pallas_call(
        fused,
        out_shape=(shape, shape),
        in_specs=[any_space] * 3 + [vmem] + [any_space] * 4
        + [vmem, pl.BlockSpec(memory_space=pltpu.SMEM)],
        out_specs=(any_space, any_space),
        scratch_shapes=scratch + [
            pltpu.SemaphoreType.DMA((7,)),
            pltpu.SemaphoreType.DMA((MESSAGES,)),
            pltpu.SemaphoreType.DMA((MESSAGES,)),
        ],
        compiler_params=pltpu.CompilerParams(
            collective_id=0, has_side_effects=True, vmem_limit_bytes=56 * 2**20
        ),
        name="sublayer",
    )(
        forward_input[0], stored_input[0], output_cotangent[0], norm_gain,
        query_weight[0], key_weight[0], value_weight[0], output_weight[0],
        frame_index.reshape(32, 128), valid_counts,
    )
    out_f, out_b = pl.pallas_call(
        hand_over,
        out_shape=(shape, shape),
        in_specs=[any_space] * 2,
        out_specs=(any_space, any_space),
        scratch_shapes=[
            pltpu.VMEM((2, ROWS, D), BF16), pltpu.SemaphoreType.DMA((4,)), pltpu.SemaphoreType.DMA((4,)),
        ],
        name="hand_over",
    )(out_f, out_b)
    return out_f[None], out_b[None]


def solution(mesh):
    return jax.shard_map(
        on_device,
        mesh=mesh,
        in_specs=(
            P("section", "seq", None),
            P("section", "seq", None),
            P("section", "seq", None),
            P("section", None),
            P("section", None, None),
            P("section", None, None),
            P("section", None, None),
            P("section", None, None),
            P(),
            P(),
        ),
        out_specs=(P("section", "seq", None), P("section", "seq", None)),
        check_vma=False,
    )
```

```python
import jax
import jax.numpy as jnp
from jax import lax
from jax.experimental import pallas as pl
from jax.experimental.pallas import tpu as pltpu
from jax.sharding import PartitionSpec as P

F32 = jnp.float32
BF16 = jnp.bfloat16
D = 1024
HEAD_DIM = 64
ROWS = 128
CHIP = 256
QROWS = 1024
KB = 512
NORM_EPSILON = 1e-05
MASKED = -1e30
FIRST_MAX = -1e20
NN = (((1,), (0,)), ((), ()))
NT = (((1,), (1,)), ((), ()))

FORWARD_ORDER = ((0, 0), (0, 1), (1, 0), (3, 0), (2, 0), (2, 1), (1, 1), (3, 1))
BACKWARD_ORDER = ((2, 1), (2, 0), (1, 1), (1, 0), (3, 1), (3, 0), (0, 1), (0, 0))
MESSAGES = 63


def dot(a, b, dims):
    return lax.dot_general(a, b, dims, preferred_element_type=F32)


def fused(
    x_f, x_b, cot_in, gain, wq_in, wk_in, wv_in, wo_in, frames, counts,
    out_f, out_b,
    xf, xb, cot, wq, wkv, wo, nb,
    kvst_b, kvst_f, kvb, kvf, aux,
    qst_b, qst_f, dost, qxb, qxf, dox,
    ws_b, ws_f, wd, wkq, wvo,
    pa, pb, sa, sb, ta, tb, ua, ub,
    acc, accq, mrow, frow,
    dkv, d0, rx, ry, dfst, dfin, part,
    ost, att, dqst, dqx, stage_f, stage_b,
    load_sem, send_sem, recv_sem,
):
    sec = lax.axis_index("section")
    seq = lax.axis_index("seq")
    n_sec = lax.axis_size("section")
    x, yh, core = seq // 8, (seq // 2) % 4, seq % 2
    other = 1 - core

    def at(xx, yy, cc):
        return {"seq": (xx * 4 + yy) * 2 + cc}

    partner = at(x, yh, other)
    xp, xm = at((x + 1) % 4, yh, core), at((x + 3) % 4, yh, core)
    yp, ym = at(x, (yh + 1) % 4, core), at(x, (yh + 3) % 4, core)
    x2, y2 = at((x + 2) % 4, yh, core), at(x, (yh + 2) % 4, core)
    sp, sm = {"section": (sec + 1) % n_sec}, {"section": (sec + n_sec - 1) % n_sec}

    loads = []
    for i, (src, dst) in enumerate((
        (x_b, xb), (wk_in, wkv.at[:, 0:128]), (wv_in, wkv.at[:, 128:256]),
        (wq_in, wq), (cot_in, cot), (wo_in, wo), (x_f, xf),
    )):
        copy = pltpu.make_async_copy(src, dst, load_sem.at[i])
        copy.start()
        loads.append(copy)

    barrier = pltpu.get_barrier_semaphore()
    for dev in (partner, xp, xm, x2, yp, ym, y2, sp, sm):
        pl.semaphore_signal(barrier, inc=1, device_id=dev, device_id_type=pl.DeviceIdType.MESH)

    used = []

    def message(src, dst, dev):
        i = len(used)
        copy = pltpu.make_async_remote_copy(
            src_ref=src, dst_ref=dst, send_sem=send_sem.at[i], recv_sem=recv_sem.at[i],
            device_id=dev, device_id_type=pl.DeviceIdType.MESH,
        )
        used.append(copy)
        return copy

    mine = pl.ds(pl.multiple_of(core * ROWS, ROWS), ROWS)

    m_kvb = message(kvst_b.at[other], kvb.at[0, 0, mine], partner)
    m_kvf = message(kvst_f.at[other], kvf.at[0, 0, mine], partner)
    m_qb = message(qst_b.at[other], qxb.at[mine], partner)
    m_qf = message(qst_f.at[other], qxf.at[mine], partner)
    m_do = message(dost.at[other], dox.at[mine], partner)
    m_att = message(ost.at[other], att.at[core], partner)
    m_dq = message(dqst.at[other], dqx.at[core], partner)
    m_dkv = message(dfst.at[other], dfin.at[core], partner)

    class Gather:
        def __init__(self, kv):
            own = kv.at[0, 0]
            self.y = (
                message(own, kv.at[3, 0], yp), message(own, kv.at[1, 0], ym),
                message(own, kv.at[2, 0], y2),
            )
            self.x = tuple(
                (message(kv.at[d, 0], kv.at[d, 2], xp), message(kv.at[d, 0], kv.at[d, 1], xm))
                for d in range(4)
            )
            self.far = {
                d: (
                    message(kv.at[d, 2, 0:128], kv.at[d, 3, 0:128], xp),
                    message(kv.at[d, 1, 128:256], kv.at[d, 3, 128:256], xm),
                )
                for d in (0, 1, 3)
            }
            self.far[2] = (message(kv.at[2, 0], kv.at[2, 3], x2),)

        def start_y(self):
            for copy in self.y:
                copy.start()

        def start_x(self, d):
            for copy in self.x[d]:
                copy.start()

        def near(self):
            self.y[0].wait_recv()
            self.start_x(3)
            self.y[1].wait_recv()
            self.start_x(1)

        def middle(self):
            self.y[2].wait_recv()
            self.start_x(2)
            self.far[2][0].start()

        def forward(self, d):
            self.x[d][0].wait_recv()
            self.far[d][0].start()
            self.x[d][1].wait_recv()
            self.far[d][1].start()

        def wait_x(self, d):
            for copy in self.x[d]:
                copy.wait_recv()

        def wait_far(self, d):
            for copy in self.far[d]:
                copy.wait_recv()

    gather_b, gather_f = Gather(kvb), Gather(kvf)

    sum_x = {
        (d, p): message(dkv.at[d, p], rx.at[d, p - 1], dev)
        for d in range(4) for p, dev in ((1, xp), (2, xm), (3, x2))
    }
    sum_y = {d: message(dkv.at[d, 0], ry.at[d - 1], dev) for d, dev in ((1, yp), (2, y2), (3, ym))}

    m_out_f = [
        message(stage_f.at[:, c:c + 512], out_f.at[:, c:c + 512], sp) for c in (0, 512)
    ]
    m_out_b = [message(stage_b.at[r:r + 64], out_b.at[r:r + 64], sm) for r in (0, 64)]
    assert len(used) == MESSAGES

    def normalize(inputs):
        wide = inputs[...].astype(F32)
        inverse = lax.rsqrt(jnp.mean(wide * wide, axis=-1, keepdims=True) + NORM_EPSILON)
        return (wide * inverse * gain[...]).astype(BF16), inverse

    def key_values(normed, staged, kv):
        both = dot(normed, wkv[...], NN)
        staged[0] = jnp.concatenate([both[:, 0:64], both[:, 128:192]], axis=1).astype(BF16)
        staged[1] = jnp.concatenate([both[:, 64:128], both[:, 192:256]], axis=1).astype(BF16)
        kv[0, 0, mine] = staged[core]

    def halves(value, staged, whole):
        staged[0] = value[:, 0:256].astype(BF16)
        staged[1] = value[:, 256:512].astype(BF16)
        whole[mine] = staged[core]

    loads[0].wait()
    normed_b, inverse_b = normalize(xb)
    nb[...] = normed_b
    loads[1].wait()
    loads[2].wait()
    key_values(nb[...], kvst_b, kvb)
    pl.semaphore_wait(barrier, 9)
    m_kvb.start()
    loads[3].wait()
    halves(dot(nb[...], wq[...], NN) * 0.125, qst_b, qxb)
    m_qb.start()
    m_kvb.wait_recv()
    gather_b.start_y()
    gather_b.start_x(0)

    loads[6].wait()
    normed_f, _ = normalize(xf)
    nb[...] = normed_f
    key_values(nb[...], kvst_f, kvf)
    m_kvf.start()
    loads[4].wait()
    loads[5].wait()
    halves(dot(cot[...], wo[...], NT), dost, dox)
    m_do.start()

    chip = x * 4 + yh

    def mask_block(k, carry):
        dy, pos = k // 4, k % 4
        dx = jnp.where(pos == 2, 3, jnp.where(pos == 3, 2, pos))
        chip_k = ((x + dx) % 4) * 4 + (yh + dy) % 4
        number = lax.broadcasted_iota(jnp.int32, (128, 128), 0)
        lane = lax.broadcasted_iota(jnp.int32, (128, 128), 1)
        for h in range(2):
            row = frames[pl.ds(2 * chip_k + h, 1), :]
            seen = (row <= number) & (lane < counts[2 * chip_k + h])
            bias = jnp.where(seen | (number >= 16), 0.0, MASKED)
            aux[dy, pos, h * 128:(h + 1) * 128, :] = bias.T.astype(BF16)
        return carry

    lax.fori_loop(0, 16, mask_block, 0)

    number = lax.broadcasted_iota(jnp.int32, (128, 128), 0)
    one_hot = jnp.concatenate(
        [(frames[pl.ds(2 * chip + h, 1), :] == number).astype(F32) for h in range(2)], axis=1
    ).astype(BF16)

    def query_operand(whole, ws):
        turned = whole[...].astype(F32).T.astype(BF16)
        for h in range(4):
            cols = pl.ds(h * CHIP, CHIP)
            ws[0:64, cols] = turned[h * 64:(h + 1) * 64, :]
            ws[64:128, cols] = jnp.zeros((64, CHIP), BF16)
            ws[128:256, cols] = one_hot

    m_qb.wait_recv()
    query_operand(qxb, ws_b)
    gather_b.forward(0)
    m_kvf.wait_recv()
    gather_f.start_x(0)
    halves(dot(nb[...], wq[...], NN) * 0.125, qst_f, qxf)
    m_qf.start()
    gather_b.near()
    gather_f.start_y()
    m_do.wait_recv()
    turned = dox[...].astype(F32).T.astype(BF16)
    nothing = jnp.zeros((CHIP, 64), F32)
    for h in range(4):
        cols = pl.ds(h * CHIP, CHIP)
        wd[0:64, cols] = jnp.zeros((64, CHIP), BF16)
        wd[64:128, cols] = turned[h * 64:(h + 1) * 64, :]
        head_q = qxb[:, h * 64:(h + 1) * 64].astype(F32)
        head_o = dox[:, h * 64:(h + 1) * 64].astype(F32)
        wkq[cols, :] = jnp.concatenate([head_q, nothing], axis=1).astype(BF16)
        wvo[cols, :] = jnp.concatenate([nothing, head_o], axis=1).astype(BF16)
    m_qf.wait_recv()
    query_operand(qxf, ws_f)

    PS, SS = (pa, pb), (sa, sb)

    def keys_of(kv, block):
        d, half = block
        return kv[d, 2 * half:2 * half + 2].reshape(KB, 128)

    def attention(kv, ws, hooks):
        acc[...] = jnp.zeros_like(acc)
        maxima = []
        lane = lax.broadcasted_iota(jnp.int32, (KB, 128), 1)
        for t in range(10):
            if t in hooks:
                hooks[t]()
            if t < 8:
                operand = jnp.concatenate(
                    [keys_of(kv, FORWARD_ORDER[t]), keys_of(aux, FORWARD_ORDER[t])], axis=1
                )
                tops = []
                for r in range(4):
                    cols = pl.ds(r * CHIP, CHIP)
                    scores = dot(operand, ws[:, cols], NN)
                    SS[t % 2][:, cols] = scores
                    tops.append(jnp.max(scores.reshape(KB // 8, 8, CHIP), axis=0))
                top = jnp.max(jnp.concatenate(tops, axis=1), axis=0, keepdims=True)
                before = maxima[-1] if maxima else jnp.full((1, QROWS), FIRST_MAX, F32)
                maxima.append(jnp.maximum(before, top))
                mrow[t:t + 1, :] = maxima[-1]
            if 1 <= t <= 8:
                n = t - 1
                for r in range(4):
                    cols = pl.ds(r * CHIP, CHIP)
                    PS[n % 2][n // 2, :, cols] = jnp.exp(
                        SS[n % 2][:, cols] - maxima[n][:, r * CHIP:(r + 1) * CHIP]
                    ).astype(BF16)
            if t >= 2:
                n = t - 2
                block = keys_of(kv, FORWARD_ORDER[n])
                turned = jnp.where(lane < 64, jnp.ones_like(block), block).T
                term = dot(turned, PS[n % 2][n // 2], NN)
                if n == 0:
                    acc[...] = term
                else:
                    acc[...] = acc[...] * jnp.exp(maxima[n - 1] - maxima[n]) + term
        return maxima[-1]

    def tokens_first(columns, staged, whole):
        tall = jnp.concatenate([columns[:, h * CHIP:(h + 1) * CHIP] for h in range(4)], axis=0)
        rows = tall.T.astype(BF16)
        staged[0] = rows[0:128]
        staged[1] = rows[128:256]
        whole[core] = staged[core]

    def second_row():
        gather_b.middle()
        gather_b.forward(1)
        gather_f.forward(0)

    def third_row():
        gather_b.forward(3)
        gather_f.near()

    final_max = attention(
        kvb, ws_b,
        {
            1: lambda: gather_b.wait_far(0),
            2: second_row,
            3: third_row,
            4: lambda: gather_b.wait_x(2),
            5: lambda: gather_b.wait_far(2),
            6: lambda: (gather_b.wait_far(1), gather_f.middle()),
            7: lambda: gather_b.wait_far(3),
        },
    )
    inverse_sum = 1.0 / acc[0:1, :]
    attended = (acc[64:128, :] * inverse_sum).astype(BF16).astype(F32)
    delta = jnp.sum(wd[64:128, :].astype(F32) * attended, axis=0, keepdims=True)
    frow[...] = jnp.exp(mrow[...] - final_max) * inverse_sum

    def add_x(d):
        whole = d0[d]
        for p in (1, 2, 3):
            sum_x[(d, p)].wait_recv()
            whole = whole + rx[d, p - 1].astype(F32)
        dkv[d, 0] = whole.astype(BF16)
        sum_y[d].start()

    TS, US = (ta, tb), (ua, ub)
    accq[...] = jnp.zeros_like(accq)

    for t in range(9):
        if t == 1:
            gather_f.forward(1)
        if t == 2:
            gather_f.forward(3)
        if t == 8:
            add_x(2)
        if t < 8:
            n = FORWARD_ORDER.index(BACKWARD_ORDER[t])
            keys = keys_of(kvb, BACKWARD_ORDER[t])
            for r in range(4):
                cols = pl.ds(r * CHIP, CHIP)
                grads = dot(keys, wd[:, cols], NN) - delta[:, r * CHIP:(r + 1) * CHIP]
                prob = PS[n % 2][n // 2, :, cols].astype(F32) * frow[n:n + 1, cols]
                TS[t % 2][:, cols] = prob.astype(BF16)
                US[t % 2][:, cols] = (prob * grads).astype(BF16)
        if t >= 1:
            d, half = BACKWARD_ORDER[t - 1]
            score_grads = US[(t - 1) % 2][...]
            accq[...] += dot(keys_of(kvb, (d, half)).T, score_grads, NN)
            terms = dot(score_grads, wkq[...], NN) + dot(TS[(t - 1) % 2][...], wvo[...], NN)
            if half == 0:
                d0[d] = terms[0:CHIP]
                dkv[d, 1] = terms[CHIP:].astype(BF16)
                sum_x[(d, 1)].start()
            else:
                dkv[d, 2] = terms[0:CHIP].astype(BF16)
                dkv[d, 3] = terms[CHIP:].astype(BF16)
                sum_x[(d, 3)].start()
                sum_x[(d, 2)].start()

    tokens_first(accq[0:64, :] * 0.125, dqst, dqx)
    m_dq.start()

    def query_part():
        m_dq.wait_recv()
        part[...] = dot(jnp.concatenate([dqx[0], dqx[1]], axis=1), wq[...], NT)

    def add_own_x():
        whole = d0[0]
        for p in (1, 2, 3):
            sum_x[(0, p)].wait_recv()
            whole = whole + rx[0, p - 1].astype(F32)
        d0[0] = whole

    def sum_own():
        whole = d0[0]
        for d in (1, 3, 2):
            sum_y[d].wait_recv()
            whole = whole + ry[d - 1].astype(F32)
        whole = whole.astype(BF16)
        dfst[0] = whole[0:128]
        dfst[1] = whole[128:256]
        dfin[core] = dfst[core]
        m_dkv.start()

    def finish_backward():
        m_dkv.wait_recv()
        first, second = dfin[0].astype(F32), dfin[1].astype(F32)
        key_value = jnp.concatenate(
            [first[:, 0:64], second[:, 0:64], first[:, 64:128], second[:, 64:128]], axis=1
        ).astype(BF16)
        for h in range(2):
            rows = pl.ds(64 * h, 64)
            grads = part[rows, :] + dot(key_value[64 * h:64 * h + 64], wkv[...], NT)
            scaled = grads * gain[...]
            wide = xb[rows, :].astype(F32)
            inverse = lax.rsqrt(jnp.mean(wide * wide, axis=-1, keepdims=True) + NORM_EPSILON)
            mean = jnp.mean(wide * scaled, axis=-1, keepdims=True)
            stage_b[rows, :] = (
                cot[rows, :].astype(F32) + inverse * scaled
                - wide * (inverse * inverse * inverse) * mean
            ).astype(BF16)
            m_out_b[h].start()

    def fourth():
        gather_f.wait_x(2)
        add_x(3)

    attention(
        kvf, ws_f,
        {
            1: lambda: (gather_f.wait_far(0), add_x(1)),
            3: query_part,
            4: fourth,
            5: lambda: gather_f.wait_far(2),
            6: lambda: gather_f.wait_far(1),
            7: lambda: gather_f.wait_far(3),
            9: add_own_x,
        },
    )
    tokens_first(acc[64:128, :] * (1.0 / acc[0:1, :]), ost, att)
    m_att.start()
    sum_own()
    m_att.wait_recv()
    attended = jnp.concatenate([att[0], att[1]], axis=1)
    for h in range(2):
        cols = pl.ds(512 * h, 512)
        stage_f[:, cols] = (
            xf[:, cols].astype(F32) + dot(attended, wo[:, cols], NN)
        ).astype(BF16)
        m_out_f[h].start()
    finish_backward()
    for copy in used:
        copy.wait_send()
    for copy in m_out_f + m_out_b:
        copy.wait_recv()


def hand_over(in_f, in_b, out_f, out_b, held, in_sem, out_sem):
    pieces = []
    for i, (src, dst) in enumerate(((in_f, out_f), (in_b, out_b))):
        for h in range(2):
            rows = pl.ds(64 * h, 64)
            arrive = pltpu.make_async_copy(src.at[rows], held.at[i, rows], in_sem.at[2 * i + h])
            leave = pltpu.make_async_copy(held.at[i, rows], dst.at[rows], out_sem.at[2 * i + h])
            arrive.start()
            pieces.append((arrive, leave))
    for arrive, leave in pieces:
        arrive.wait()
        leave.start()
    for _, leave in pieces:
        leave.wait()


def on_device(
    forward_input, stored_input, output_cotangent, norm_gain,
    query_weight, key_weight, value_weight, output_weight, frame_index, valid_counts,
):
    any_space = pl.BlockSpec(memory_space=pl.ANY)
    vmem = pl.BlockSpec(memory_space=pltpu.VMEM)
    shape = jax.ShapeDtypeStruct((ROWS, D), BF16)
    scratch = [
        (ROWS, D), (ROWS, D), (ROWS, D), (D, 512), (D, 256), (512, D), (ROWS, D),
        (2, ROWS, 128), (2, ROWS, 128), (4, 4, CHIP, 128), (4, 4, CHIP, 128), (4, 4, CHIP, 128),
        (2, ROWS, 256), (2, ROWS, 256), (2, ROWS, 256), (CHIP, 256), (CHIP, 256), (CHIP, 256),
        (256, QROWS), (256, QROWS), (128, QROWS), (QROWS, 128), (QROWS, 128),
        (4, KB, QROWS), (4, KB, QROWS), ((KB, QROWS), F32), ((KB, QROWS), F32),
        (KB, QROWS), (KB, QROWS), (KB, QROWS), (KB, QROWS),
        ((128, QROWS), F32), ((128, QROWS), F32), ((8, QROWS), F32), ((8, QROWS), F32),
        (4, 4, CHIP, 128), ((4, CHIP, 128), F32), (4, 3, CHIP, 128), (3, CHIP, 128),
        (2, ROWS, 128), (2, ROWS, 128), ((ROWS, D), F32),
        (2, ROWS, 256), (2, ROWS, 256), (2, ROWS, 256), (2, ROWS, 256), (ROWS, D), (ROWS, D),
    ]
    scratch = [
        pltpu.VMEM(*s) if isinstance(s[1], type) or not isinstance(s[1], int) else pltpu.VMEM(s, BF16)
        for s in scratch
    ]
    out_f, out_b = pl.pallas_call(
        fused,
        out_shape=(shape, shape),
        in_specs=[any_space] * 3 + [vmem] + [any_space] * 4
        + [vmem, pl.BlockSpec(memory_space=pltpu.SMEM)],
        out_specs=(any_space, any_space),
        scratch_shapes=scratch + [
            pltpu.SemaphoreType.DMA((7,)),
            pltpu.SemaphoreType.DMA((MESSAGES,)),
            pltpu.SemaphoreType.DMA((MESSAGES,)),
        ],
        compiler_params=pltpu.CompilerParams(
            collective_id=0, has_side_effects=True, vmem_limit_bytes=56 * 2**20
        ),
        name="sublayer",
    )(
        forward_input[0], stored_input[0], output_cotangent[0], norm_gain,
        query_weight[0], key_weight[0], value_weight[0], output_weight[0],
        frame_index.reshape(32, 128), valid_counts,
    )
    out_f, out_b = pl.pallas_call(
        hand_over,
        out_shape=(shape, shape),
        in_specs=[any_space] * 2,
        out_specs=(any_space, any_space),
        scratch_shapes=[
            pltpu.VMEM((2, ROWS, D), BF16), pltpu.SemaphoreType.DMA((4,)), pltpu.SemaphoreType.DMA((4,)),
        ],
        name="hand_over",
    )(out_f, out_b)
    return out_f[None], out_b[None]


def solution(mesh):
    return jax.shard_map(
        on_device,
        mesh=mesh,
        in_specs=(
            P("section", "seq", None),
            P("section", "seq", None),
            P("section", "seq", None),
            P("section", None),
            P("section", None, None),
            P("section", None, None),
            P("section", None, None),
            P("section", None, None),
            P(),
            P(),
        ),
        out_specs=(P("section", "seq", None), P("section", "seq", None)),
        check_vma=False,
    )
```

```python
import jax
import jax.numpy as jnp
from jax import lax
from jax.experimental import pallas as pl
from jax.experimental.pallas import tpu as pltpu
from jax.sharding import PartitionSpec as P

F32 = jnp.float32
BF16 = jnp.bfloat16
D = 1024
HEAD_DIM = 64
ROWS = 128
CHIP = 256
QROWS = 1024
KB = 512
NORM_EPSILON = 1e-05
MASKED = -1e30
FIRST_MAX = -1e20
NN = (((1,), (0,)), ((), ()))
NT = (((1,), (1,)), ((), ()))

FORWARD_ORDER = ((0, 0), (0, 1), (1, 0), (3, 0), (2, 0), (2, 1), (1, 1), (3, 1))
BACKWARD_ORDER = ((2, 1), (2, 0), (1, 1), (1, 0), (3, 1), (3, 0), (0, 1), (0, 0))
MESSAGES = 57


def dot(a, b, dims):
    return lax.dot_general(a, b, dims, preferred_element_type=F32)


def fused(
    x_f, x_b, cot_in, gain, wq_in, wk_in, wv_in, wo_in, frames, counts,
    out_f, out_b,
    xf, xb, cot, wq, wkv, wo, nb,
    kvst_b, kvst_f, kvb, kvf, aux,
    qst_b, qst_f, dost, qxb, qxf, dox,
    ws_b, ws_f, wd, wkq, wvo,
    pa, pb, sa, sb, ta, tb, ua, ub,
    acc, accq, mrow, frow,
    dkv, d0, rx, ry, dfst, dfin, part,
    ost, att, dqst, dqx, stage_f, stage_b,
    load_sem, send_sem, recv_sem,
):
    sec = lax.axis_index("section")
    seq = lax.axis_index("seq")
    n_sec = lax.axis_size("section")
    x, yh, core = seq // 8, (seq // 2) % 4, seq % 2
    other = 1 - core

    def at(xx, yy, cc):
        return {"seq": (xx * 4 + yy) * 2 + cc}

    partner = at(x, yh, other)
    xp, xm = at((x + 1) % 4, yh, core), at((x + 3) % 4, yh, core)
    yp, ym = at(x, (yh + 1) % 4, core), at(x, (yh + 3) % 4, core)
    x2, y2 = at((x + 2) % 4, yh, core), at(x, (yh + 2) % 4, core)
    sp, sm = {"section": (sec + 1) % n_sec}, {"section": (sec + n_sec - 1) % n_sec}

    loads = []
    for i, (src, dst) in enumerate((
        (x_b, xb), (wk_in, wkv.at[:, 0:128]), (wv_in, wkv.at[:, 128:256]),
        (wq_in, wq), (cot_in, cot), (wo_in, wo), (x_f, xf),
    )):
        copy = pltpu.make_async_copy(src, dst, load_sem.at[i])
        copy.start()
        loads.append(copy)

    barrier = pltpu.get_barrier_semaphore()
    for dev in (partner, xp, xm, x2, yp, ym, y2, sp, sm):
        pl.semaphore_signal(barrier, inc=1, device_id=dev, device_id_type=pl.DeviceIdType.MESH)

    used = []

    def message(src, dst, dev):
        i = len(used)
        copy = pltpu.make_async_remote_copy(
            src_ref=src, dst_ref=dst, send_sem=send_sem.at[i], recv_sem=recv_sem.at[i],
            device_id=dev, device_id_type=pl.DeviceIdType.MESH,
        )
        used.append(copy)
        return copy

    mine = pl.ds(pl.multiple_of(core * ROWS, ROWS), ROWS)

    m_kvb = message(kvst_b.at[other], kvb.at[0, 0, mine], partner)
    m_kvf = message(kvst_f.at[other], kvf.at[0, 0, mine], partner)
    m_qb = message(qst_b.at[other], qxb.at[mine], partner)
    m_qf = message(qst_f.at[other], qxf.at[mine], partner)
    m_do = message(dost.at[other], dox.at[mine], partner)
    m_att = message(ost.at[other], att.at[core], partner)
    m_dq = message(dqst.at[other], dqx.at[core], partner)
    m_dkv = message(dfst.at[other], dfin.at[core], partner)

    class Gather:
        def __init__(self, kv):
            own = kv.at[0, 0]
            self.y = (
                message(own, kv.at[3, 0], yp), message(own, kv.at[1, 0], ym),
                message(own, kv.at[2, 0], y2),
            )
            self.x = tuple(
                (message(kv.at[d, 0], kv.at[d, 2], xp), message(kv.at[d, 0], kv.at[d, 1], xm))
                for d in range(4)
            )
            self.far = {
                d: (
                    message(kv.at[d, 2, 0:128], kv.at[d, 3, 0:128], xp),
                    message(kv.at[d, 1, 128:256], kv.at[d, 3, 128:256], xm),
                )
                for d in (0, 1, 3)
            }
            self.far[2] = (message(kv.at[2, 0], kv.at[2, 3], x2),)

        def start_y(self):
            for copy in self.y:
                copy.start()

        def start_x(self, d):
            for copy in self.x[d]:
                copy.start()

        def near(self):
            self.y[0].wait_recv()
            self.start_x(3)
            self.y[1].wait_recv()
            self.start_x(1)

        def middle(self):
            self.y[2].wait_recv()
            self.start_x(2)
            self.far[2][0].start()

        def forward(self, d):
            self.x[d][0].wait_recv()
            self.far[d][0].start()
            self.x[d][1].wait_recv()
            self.far[d][1].start()

        def wait_x(self, d):
            for copy in self.x[d]:
                copy.wait_recv()

        def wait_far(self, d):
            for copy in self.far[d]:
                copy.wait_recv()

    class WideGather:
        def __init__(self, kv):
            own = kv.at[0, 0]
            self.y = (
                message(own, kv.at[3, 0], yp), message(own, kv.at[1, 0], ym),
                message(own, kv.at[2, 0], y2),
            )
            self.x = (message(own, kv.at[0, 2], xp), message(own, kv.at[0, 1], xm))
            self.far = (
                message(kv.at[0, 2, 0:128], kv.at[0, 3, 0:128], xp),
                message(kv.at[0, 1, 128:256], kv.at[0, 3, 128:256], xm),
            )
            self.row = (
                message(kv.at[0, 1:4], kv.at[3, 1:4], yp), message(kv.at[0, 1:4], kv.at[1, 1:4], ym),
            )
            self.across = (
                message(kv.at[2, 0], kv.at[2, 2], xp), message(kv.at[2, 0], kv.at[2, 1], xm),
                message(kv.at[2, 0], kv.at[2, 3], x2),
            )

        def start_y(self):
            for copy in self.y:
                copy.start()

        def start_x(self):
            for copy in self.x:
                copy.start()

        def forward(self):
            for near, far in zip(self.x, self.far):
                near.wait_recv()
                far.start()

        def start_row(self):
            for copy in self.far:
                copy.wait_recv()
            for copy in self.row:
                copy.start()

        def middle(self):
            self.y[2].wait_recv()
            for copy in self.across:
                copy.start()

        def wait_row(self, i):
            self.y[i].wait_recv()
            self.row[i].wait_recv()

        def wait_across(self):
            for copy in self.across:
                copy.wait_recv()

    gather_b, gather_f = Gather(kvb), WideGather(kvf)

    sum_x = {
        (d, p): message(dkv.at[d, p], rx.at[d, p - 1], dev)
        for d in range(4) for p, dev in ((1, xp), (2, xm), (3, x2))
    }
    sum_y = {d: message(dkv.at[d, 0], ry.at[d - 1], dev) for d, dev in ((1, yp), (2, y2), (3, ym))}

    m_out_f = [
        message(stage_f.at[:, c:c + 512], out_f.at[:, c:c + 512], sp) for c in (0, 512)
    ]
    m_out_b = [message(stage_b.at[r:r + 64], out_b.at[r:r + 64], sm) for r in (0, 64)]
    assert len(used) == MESSAGES

    def normalize(inputs):
        wide = inputs[...].astype(F32)
        inverse = lax.rsqrt(jnp.mean(wide * wide, axis=-1, keepdims=True) + NORM_EPSILON)
        return (wide * inverse * gain[...]).astype(BF16), inverse

    def key_values(normed, staged, kv):
        both = dot(normed, wkv[...], NN)
        staged[0] = jnp.concatenate([both[:, 0:64], both[:, 128:192]], axis=1).astype(BF16)
        staged[1] = jnp.concatenate([both[:, 64:128], both[:, 192:256]], axis=1).astype(BF16)
        kv[0, 0, mine] = staged[core]

    def halves(value, staged, whole):
        staged[0] = value[:, 0:256].astype(BF16)
        staged[1] = value[:, 256:512].astype(BF16)
        whole[mine] = staged[core]

    loads[0].wait()
    normed_b, inverse_b = normalize(xb)
    nb[...] = normed_b
    loads[1].wait()
    loads[2].wait()
    key_values(nb[...], kvst_b, kvb)
    pl.semaphore_wait(barrier, 9)
    m_kvb.start()
    loads[3].wait()
    halves(dot(nb[...], wq[...], NN) * 0.125, qst_b, qxb)
    m_qb.start()
    m_kvb.wait_recv()
    gather_b.start_y()
    gather_b.start_x(0)

    loads[6].wait()
    normed_f, _ = normalize(xf)
    nb[...] = normed_f
    key_values(nb[...], kvst_f, kvf)
    m_kvf.start()
    loads[4].wait()
    loads[5].wait()
    halves(dot(cot[...], wo[...], NT), dost, dox)
    m_do.start()

    chip = x * 4 + yh

    def mask_block(k, carry):
        dy, pos = k // 4, k % 4
        dx = jnp.where(pos == 2, 3, jnp.where(pos == 3, 2, pos))
        chip_k = ((x + dx) % 4) * 4 + (yh + dy) % 4
        number = lax.broadcasted_iota(jnp.int32, (128, 128), 0)
        lane = lax.broadcasted_iota(jnp.int32, (128, 128), 1)
        for h in range(2):
            row = frames[pl.ds(2 * chip_k + h, 1), :]
            seen = (row <= number) & (lane < counts[2 * chip_k + h])
            bias = jnp.where(seen | (number >= 16), 0.0, MASKED)
            aux[dy, pos, h * 128:(h + 1) * 128, :] = bias.T.astype(BF16)
        return carry

    lax.fori_loop(0, 16, mask_block, 0)

    number = lax.broadcasted_iota(jnp.int32, (128, 128), 0)
    one_hot = jnp.concatenate(
        [(frames[pl.ds(2 * chip + h, 1), :] == number).astype(F32) for h in range(2)], axis=1
    ).astype(BF16)

    def query_operand(whole, ws):
        turned = whole[...].astype(F32).T.astype(BF16)
        for h in range(4):
            cols = pl.ds(h * CHIP, CHIP)
            ws[0:64, cols] = turned[h * 64:(h + 1) * 64, :]
            ws[64:128, cols] = jnp.zeros((64, CHIP), BF16)
            ws[128:256, cols] = one_hot

    m_qb.wait_recv()
    query_operand(qxb, ws_b)
    gather_b.forward(0)
    m_kvf.wait_recv()
    gather_f.start_x()
    halves(dot(nb[...], wq[...], NN) * 0.125, qst_f, qxf)
    m_qf.start()
    gather_b.near()
    gather_f.start_y()
    m_do.wait_recv()
    turned = dox[...].astype(F32).T.astype(BF16)
    nothing = jnp.zeros((CHIP, 64), F32)
    for h in range(4):
        cols = pl.ds(h * CHIP, CHIP)
        wd[0:64, cols] = jnp.zeros((64, CHIP), BF16)
        wd[64:128, cols] = turned[h * 64:(h + 1) * 64, :]
        head_q = qxb[:, h * 64:(h + 1) * 64].astype(F32)
        head_o = dox[:, h * 64:(h + 1) * 64].astype(F32)
        wkq[cols, :] = jnp.concatenate([head_q, nothing], axis=1).astype(BF16)
        wvo[cols, :] = jnp.concatenate([nothing, head_o], axis=1).astype(BF16)
    m_qf.wait_recv()
    query_operand(qxf, ws_f)

    PS, SS = (pa, pb), (sa, sb)

    def keys_of(kv, block):
        d, half = block
        return kv[d, 2 * half:2 * half + 2].reshape(KB, 128)

    def attention(kv, ws, hooks):
        acc[...] = jnp.zeros_like(acc)
        maxima = []
        lane = lax.broadcasted_iota(jnp.int32, (KB, 128), 1)
        for t in range(10):
            if t in hooks:
                hooks[t]()
            if t < 8:
                operand = jnp.concatenate(
                    [keys_of(kv, FORWARD_ORDER[t]), keys_of(aux, FORWARD_ORDER[t])], axis=1
                )
                tops = []
                for r in range(4):
                    cols = pl.ds(r * CHIP, CHIP)
                    scores = dot(operand, ws[:, cols], NN)
                    SS[t % 2][:, cols] = scores
                    tops.append(jnp.max(scores.reshape(KB // 8, 8, CHIP), axis=0))
                top = jnp.max(jnp.concatenate(tops, axis=1), axis=0, keepdims=True)
                before = maxima[-1] if maxima else jnp.full((1, QROWS), FIRST_MAX, F32)
                maxima.append(jnp.maximum(before, top))
                mrow[t:t + 1, :] = maxima[-1]
            if 1 <= t <= 8:
                n = t - 1
                for r in range(4):
                    cols = pl.ds(r * CHIP, CHIP)
                    PS[n % 2][n // 2, :, cols] = jnp.exp(
                        SS[n % 2][:, cols] - maxima[n][:, r * CHIP:(r + 1) * CHIP]
                    ).astype(BF16)
            if t >= 2:
                n = t - 2
                block = keys_of(kv, FORWARD_ORDER[n])
                turned = jnp.where(lane < 64, jnp.ones_like(block), block).T
                term = dot(turned, PS[n % 2][n // 2], NN)
                if n == 0:
                    acc[...] = term
                else:
                    acc[...] = acc[...] * jnp.exp(maxima[n - 1] - maxima[n]) + term
        return maxima[-1]

    def tokens_first(columns, staged, whole):
        tall = jnp.concatenate([columns[:, h * CHIP:(h + 1) * CHIP] for h in range(4)], axis=0)
        rows = tall.T.astype(BF16)
        staged[0] = rows[0:128]
        staged[1] = rows[128:256]
        whole[core] = staged[core]

    final_max = attention(
        kvb, ws_b,
        {
            1: lambda: (gather_b.wait_far(0), gather_f.forward()),
            2: lambda: (gather_b.middle(), gather_b.forward(1)),
            3: lambda: gather_b.forward(3),
            4: lambda: (gather_b.wait_x(2), gather_f.start_row()),
            5: lambda: gather_b.wait_far(2),
            6: lambda: (gather_b.wait_far(1), gather_f.middle()),
            7: lambda: gather_b.wait_far(3),
        },
    )
    inverse_sum = 1.0 / acc[0:1, :]
    attended = (acc[64:128, :] * inverse_sum).astype(BF16).astype(F32)
    delta = jnp.sum(wd[64:128, :].astype(F32) * attended, axis=0, keepdims=True)
    frow[...] = jnp.exp(mrow[...] - final_max) * inverse_sum

    def add_x(d):
        whole = d0[d]
        for p in (1, 2, 3):
            sum_x[(d, p)].wait_recv()
            whole = whole + rx[d, p - 1].astype(F32)
        dkv[d, 0] = whole.astype(BF16)
        sum_y[d].start()

    TS, US = (ta, tb), (ua, ub)
    accq[...] = jnp.zeros_like(accq)

    for t in range(9):
        if t == 8:
            add_x(2)
        if t < 8:
            n = FORWARD_ORDER.index(BACKWARD_ORDER[t])
            keys = keys_of(kvb, BACKWARD_ORDER[t])
            for r in range(4):
                cols = pl.ds(r * CHIP, CHIP)
                grads = dot(keys, wd[:, cols], NN) - delta[:, r * CHIP:(r + 1) * CHIP]
                prob = PS[n % 2][n // 2, :, cols].astype(F32) * frow[n:n + 1, cols]
                TS[t % 2][:, cols] = prob.astype(BF16)
                US[t % 2][:, cols] = (prob * grads).astype(BF16)
        if t >= 1:
            d, half = BACKWARD_ORDER[t - 1]
            score_grads = US[(t - 1) % 2][...]
            accq[...] += dot(keys_of(kvb, (d, half)).T, score_grads, NN)
            terms = dot(score_grads, wkq[...], NN) + dot(TS[(t - 1) % 2][...], wvo[...], NN)
            if half == 0:
                d0[d] = terms[0:CHIP]
                dkv[d, 1] = terms[CHIP:].astype(BF16)
                sum_x[(d, 1)].start()
            else:
                dkv[d, 2] = terms[0:CHIP].astype(BF16)
                dkv[d, 3] = terms[CHIP:].astype(BF16)
                sum_x[(d, 3)].start()
                sum_x[(d, 2)].start()

    tokens_first(accq[0:64, :] * 0.125, dqst, dqx)
    m_dq.start()

    def query_part():
        m_dq.wait_recv()
        part[...] = dot(jnp.concatenate([dqx[0], dqx[1]], axis=1), wq[...], NT)

    def add_own_x():
        whole = d0[0]
        for p in (1, 2, 3):
            sum_x[(0, p)].wait_recv()
            whole = whole + rx[0, p - 1].astype(F32)
        d0[0] = whole

    def sum_own():
        whole = d0[0]
        for d in (1, 3, 2):
            sum_y[d].wait_recv()
            whole = whole + ry[d - 1].astype(F32)
        whole = whole.astype(BF16)
        dfst[0] = whole[0:128]
        dfst[1] = whole[128:256]
        dfin[core] = dfst[core]
        m_dkv.start()

    def finish_backward():
        m_dkv.wait_recv()
        first, second = dfin[0].astype(F32), dfin[1].astype(F32)
        key_value = jnp.concatenate(
            [first[:, 0:64], second[:, 0:64], first[:, 64:128], second[:, 64:128]], axis=1
        ).astype(BF16)
        for h in range(2):
            rows = pl.ds(64 * h, 64)
            grads = part[rows, :] + dot(key_value[64 * h:64 * h + 64], wkv[...], NT)
            scaled = grads * gain[...]
            wide = xb[rows, :].astype(F32)
            inverse = lax.rsqrt(jnp.mean(wide * wide, axis=-1, keepdims=True) + NORM_EPSILON)
            mean = jnp.mean(wide * scaled, axis=-1, keepdims=True)
            stage_b[rows, :] = (
                cot[rows, :].astype(F32) + inverse * scaled
                - wide * (inverse * inverse * inverse) * mean
            ).astype(BF16)
            m_out_b[h].start()

    attention(
        kvf, ws_f,
        {
            1: lambda: add_x(1),
            2: lambda: gather_f.wait_row(1),
            3: lambda: (gather_f.wait_row(0), query_part()),
            4: lambda: (gather_f.wait_across(), add_x(3)),
            9: add_own_x,
        },
    )
    tokens_first(acc[64:128, :] * (1.0 / acc[0:1, :]), ost, att)
    m_att.start()
    sum_own()
    m_att.wait_recv()
    attended = jnp.concatenate([att[0], att[1]], axis=1)
    for h in range(2):
        cols = pl.ds(512 * h, 512)
        stage_f[:, cols] = (
            xf[:, cols].astype(F32) + dot(attended, wo[:, cols], NN)
        ).astype(BF16)
        m_out_f[h].start()
    finish_backward()
    for copy in used:
        copy.wait_send()
    for copy in m_out_f + m_out_b:
        copy.wait_recv()


def hand_over(in_f, in_b, out_f, out_b, held, in_sem, out_sem):
    pieces = []
    for i, (src, dst) in enumerate(((in_f, out_f), (in_b, out_b))):
        for h in range(2):
            rows = pl.ds(64 * h, 64)
            arrive = pltpu.make_async_copy(src.at[rows], held.at[i, rows], in_sem.at[2 * i + h])
            leave = pltpu.make_async_copy(held.at[i, rows], dst.at[rows], out_sem.at[2 * i + h])
            arrive.start()
            pieces.append((arrive, leave))
    for arrive, leave in pieces:
        arrive.wait()
        leave.start()
    for _, leave in pieces:
        leave.wait()


def on_device(
    forward_input, stored_input, output_cotangent, norm_gain,
    query_weight, key_weight, value_weight, output_weight, frame_index, valid_counts,
):
    any_space = pl.BlockSpec(memory_space=pl.ANY)
    vmem = pl.BlockSpec(memory_space=pltpu.VMEM)
    shape = jax.ShapeDtypeStruct((ROWS, D), BF16)
    scratch = [
        (ROWS, D), (ROWS, D), (ROWS, D), (D, 512), (D, 256), (512, D), (ROWS, D),
        (2, ROWS, 128), (2, ROWS, 128), (4, 4, CHIP, 128), (4, 4, CHIP, 128), (4, 4, CHIP, 128),
        (2, ROWS, 256), (2, ROWS, 256), (2, ROWS, 256), (CHIP, 256), (CHIP, 256), (CHIP, 256),
        (256, QROWS), (256, QROWS), (128, QROWS), (QROWS, 128), (QROWS, 128),
        (4, KB, QROWS), (4, KB, QROWS), ((KB, QROWS), F32), ((KB, QROWS), F32),
        (KB, QROWS), (KB, QROWS), (KB, QROWS), (KB, QROWS),
        ((128, QROWS), F32), ((128, QROWS), F32), ((8, QROWS), F32), ((8, QROWS), F32),
        (4, 4, CHIP, 128), ((4, CHIP, 128), F32), (4, 3, CHIP, 128), (3, CHIP, 128),
        (2, ROWS, 128), (2, ROWS, 128), ((ROWS, D), F32),
        (2, ROWS, 256), (2, ROWS, 256), (2, ROWS, 256), (2, ROWS, 256), (ROWS, D), (ROWS, D),
    ]
    scratch = [
        pltpu.VMEM(*s) if isinstance(s[1], type) or not isinstance(s[1], int) else pltpu.VMEM(s, BF16)
        for s in scratch
    ]
    out_f, out_b = pl.pallas_call(
        fused,
        out_shape=(shape, shape),
        in_specs=[any_space] * 3 + [vmem] + [any_space] * 4
        + [vmem, pl.BlockSpec(memory_space=pltpu.SMEM)],
        out_specs=(any_space, any_space),
        scratch_shapes=scratch + [
            pltpu.SemaphoreType.DMA((7,)),
            pltpu.SemaphoreType.DMA((MESSAGES,)),
            pltpu.SemaphoreType.DMA((MESSAGES,)),
        ],
        compiler_params=pltpu.CompilerParams(
            collective_id=0, has_side_effects=True, vmem_limit_bytes=56 * 2**20
        ),
        name="sublayer",
    )(
        forward_input[0], stored_input[0], output_cotangent[0], norm_gain,
        query_weight[0], key_weight[0], value_weight[0], output_weight[0],
        frame_index.reshape(32, 128), valid_counts,
    )
    out_f, out_b = pl.pallas_call(
        hand_over,
        out_shape=(shape, shape),
        in_specs=[any_space] * 2,
        out_specs=(any_space, any_space),
        scratch_shapes=[
            pltpu.VMEM((2, ROWS, D), BF16), pltpu.SemaphoreType.DMA((4,)), pltpu.SemaphoreType.DMA((4,)),
        ],
        name="hand_over",
    )(out_f, out_b)
    return out_f[None], out_b[None]


def solution(mesh):
    return jax.shard_map(
        on_device,
        mesh=mesh,
        in_specs=(
            P("section", "seq", None),
            P("section", "seq", None),
            P("section", "seq", None),
            P("section", None),
            P("section", None, None),
            P("section", None, None),
            P("section", None, None),
            P("section", None, None),
            P(),
            P(),
        ),
        out_specs=(P("section", "seq", None), P("section", "seq", None)),
        check_vma=False,
    )
```

```python
import jax
import jax.numpy as jnp
from jax import lax
from jax.experimental import pallas as pl
from jax.experimental.pallas import tpu as pltpu
from jax.sharding import PartitionSpec as P

F32 = jnp.float32
BF16 = jnp.bfloat16
D = 1024
HEAD_DIM = 64
ROWS = 128
CHIP = 256
QROWS = 1024
KB = 512
NORM_EPSILON = 1e-05
MASKED = -1e30
FIRST_MAX = -1e20
NN = (((1,), (0,)), ((), ()))
NT = (((1,), (1,)), ((), ()))

FORWARD_ORDER = ((0, 0), (0, 1), (1, 0), (3, 0), (2, 0), (2, 1), (1, 1), (3, 1))
BACKWARD_ORDER = ((2, 1), (2, 0), (1, 1), (1, 0), (3, 1), (3, 0), (0, 1), (0, 0))
MESSAGES = 63


def dot(a, b, dims):
    return lax.dot_general(a, b, dims, preferred_element_type=F32)


def fused(
    x_f, x_b, cot_in, gain, wq_in, wk_in, wv_in, wo_in, frames, counts,
    out_f, out_b,
    xf, xb, cot, wq, wkv, wo, nb,
    kvst_b, kvst_f, kvb, kvf, aux,
    qst_b, qst_f, dost, qxb, qxf, dox,
    ws_b, ws_f, wd, wkq, wvo,
    pa, pb, sa, sb, ta, tb, ua, ub,
    acc, accq, mrow, frow,
    dkv, d0, rx, ry, dfst, dfin, part,
    ost, att, dqst, dqx, stage_f, stage_b,
    load_sem, send_sem, recv_sem,
):
    sec = lax.axis_index("section")
    seq = lax.axis_index("seq")
    n_sec = lax.axis_size("section")
    x, yh, core = seq // 8, (seq // 2) % 4, seq % 2
    other = 1 - core

    def at(xx, yy, cc):
        return {"seq": (xx * 4 + yy) * 2 + cc}

    partner = at(x, yh, other)
    xp, xm = at((x + 1) % 4, yh, core), at((x + 3) % 4, yh, core)
    yp, ym = at(x, (yh + 1) % 4, core), at(x, (yh + 3) % 4, core)
    x2, y2 = at((x + 2) % 4, yh, core), at(x, (yh + 2) % 4, core)
    sp, sm = {"section": (sec + 1) % n_sec}, {"section": (sec + n_sec - 1) % n_sec}

    loads = []
    for i, (src, dst) in enumerate((
        (x_b, xb), (wk_in, wkv.at[:, 0:128]), (wv_in, wkv.at[:, 128:256]),
        (wq_in, wq), (cot_in, cot), (wo_in, wo), (x_f, xf),
    )):
        copy = pltpu.make_async_copy(src, dst, load_sem.at[i])
        copy.start()
        loads.append(copy)

    barrier = pltpu.get_barrier_semaphore()
    for dev in (partner, xp, xm, x2, yp, ym, y2, sp, sm):
        pl.semaphore_signal(barrier, inc=1, device_id=dev, device_id_type=pl.DeviceIdType.MESH)

    used = []

    def message(src, dst, dev):
        i = len(used)
        copy = pltpu.make_async_remote_copy(
            src_ref=src, dst_ref=dst, send_sem=send_sem.at[i], recv_sem=recv_sem.at[i],
            device_id=dev, device_id_type=pl.DeviceIdType.MESH,
        )
        used.append(copy)
        return copy

    mine = pl.ds(pl.multiple_of(core * ROWS, ROWS), ROWS)

    m_kvb = message(kvst_b.at[other], kvb.at[0, 0, mine], partner)
    m_kvf = message(kvst_f.at[other], kvf.at[0, 0, mine], partner)
    m_qb = message(qst_b.at[other], qxb.at[mine], partner)
    m_qf = message(qst_f.at[other], qxf.at[mine], partner)
    m_do = message(dost.at[other], dox.at[mine], partner)
    m_att = message(ost.at[other], att.at[core], partner)
    m_dq = message(dqst.at[other], dqx.at[core], partner)
    m_dkv = message(dfst.at[other], dfin.at[core], partner)

    class Gather:
        def __init__(self, kv):
            own = kv.at[0, 0]
            self.y = (
                message(own, kv.at[3, 0], yp), message(own, kv.at[1, 0], ym),
                message(own, kv.at[2, 0], y2),
            )
            self.x = tuple(
                (message(kv.at[d, 0], kv.at[d, 2], xp), message(kv.at[d, 0], kv.at[d, 1], xm))
                for d in range(4)
            )
            self.far = {
                d: (
                    message(kv.at[d, 2, 0:128], kv.at[d, 3, 0:128], xp),
                    message(kv.at[d, 1, 128:256], kv.at[d, 3, 128:256], xm),
                )
                for d in (0, 1, 3)
            }
            self.far[2] = (message(kv.at[2, 0], kv.at[2, 3], x2),)

        def start_y(self):
            for copy in self.y:
                copy.start()

        def start_x(self, d):
            for copy in self.x[d]:
                copy.start()

        def near(self):
            self.y[0].wait_recv()
            self.start_x(3)
            self.y[1].wait_recv()
            self.start_x(1)

        def middle(self):
            self.y[2].wait_recv()
            self.start_x(2)
            self.far[2][0].start()

        def forward(self, d):
            self.x[d][0].wait_recv()
            self.far[d][0].start()
            self.x[d][1].wait_recv()
            self.far[d][1].start()

        def wait_x(self, d):
            for copy in self.x[d]:
                copy.wait_recv()

        def wait_far(self, d):
            for copy in self.far[d]:
                copy.wait_recv()

    gather_b, gather_f = Gather(kvb), Gather(kvf)

    sum_x = {
        (d, p): message(dkv.at[d, p], rx.at[d, p - 1], dev)
        for d in range(4) for p, dev in ((1, xp), (2, xm), (3, x2))
    }
    sum_y = {d: message(dkv.at[d, 0], ry.at[d - 1], dev) for d, dev in ((1, yp), (2, y2), (3, ym))}

    m_out_f = [
        message(stage_f.at[:, c:c + 512], out_f.at[:, c:c + 512], sp) for c in (0, 512)
    ]
    m_out_b = [message(stage_b.at[r:r + 64], out_b.at[r:r + 64], sm) for r in (0, 64)]
    assert len(used) == MESSAGES

    def normalize(inputs):
        wide = inputs[...].astype(F32)
        inverse = lax.rsqrt(jnp.mean(wide * wide, axis=-1, keepdims=True) + NORM_EPSILON)
        return (wide * inverse * gain[...]).astype(BF16), inverse

    def key_values(normed, staged, kv):
        both = dot(normed, wkv[...], NN)
        staged[0] = jnp.concatenate([both[:, 0:64], both[:, 128:192]], axis=1).astype(BF16)
        staged[1] = jnp.concatenate([both[:, 64:128], both[:, 192:256]], axis=1).astype(BF16)
        kv[0, 0, mine] = staged[core]

    def halves(value, staged, whole):
        staged[0] = value[:, 0:256].astype(BF16)
        staged[1] = value[:, 256:512].astype(BF16)
        whole[mine] = staged[core]

    loads[0].wait()
    normed_b, inverse_b = normalize(xb)
    nb[...] = normed_b
    loads[1].wait()
    loads[2].wait()
    key_values(nb[...], kvst_b, kvb)
    pl.semaphore_wait(barrier, 9)
    m_kvb.start()
    loads[3].wait()
    halves(dot(nb[...], wq[...], NN) * 0.125, qst_b, qxb)
    m_qb.start()
    m_kvb.wait_recv()
    gather_b.start_y()
    gather_b.start_x(0)

    loads[6].wait()
    normed_f, _ = normalize(xf)
    nb[...] = normed_f
    key_values(nb[...], kvst_f, kvf)
    m_kvf.start()
    loads[4].wait()
    loads[5].wait()
    halves(dot(cot[...], wo[...], NT), dost, dox)
    m_do.start()

    chip = x * 4 + yh

    def mask_block(k, carry):
        dy, pos = k // 4, k % 4
        dx = jnp.where(pos == 2, 3, jnp.where(pos == 3, 2, pos))
        chip_k = ((x + dx) % 4) * 4 + (yh + dy) % 4
        number = lax.broadcasted_iota(jnp.int32, (128, 128), 0)
        lane = lax.broadcasted_iota(jnp.int32, (128, 128), 1)
        for h in range(2):
            row = frames[pl.ds(2 * chip_k + h, 1), :]
            seen = (row <= number) & (lane < counts[2 * chip_k + h])
            bias = jnp.where(seen | (number >= 16), 0.0, MASKED)
            aux[dy, pos, h * 128:(h + 1) * 128, :] = bias.T.astype(BF16)
        return carry

    lax.fori_loop(0, 16, mask_block, 0)

    number = lax.broadcasted_iota(jnp.int32, (128, 128), 0)
    one_hot = jnp.concatenate(
        [(frames[pl.ds(2 * chip + h, 1), :] == number).astype(F32) for h in range(2)], axis=1
    ).astype(BF16)

    def query_operand(whole, ws):
        turned = whole[...].astype(F32).T.astype(BF16)
        for h in range(4):
            cols = pl.ds(h * CHIP, CHIP)
            ws[0:64, cols] = turned[h * 64:(h + 1) * 64, :]
            ws[64:128, cols] = jnp.zeros((64, CHIP), BF16)
            ws[128:256, cols] = one_hot

    m_qb.wait_recv()
    query_operand(qxb, ws_b)
    gather_b.forward(0)
    m_kvf.wait_recv()
    gather_f.start_x(0)
    halves(dot(nb[...], wq[...], NN) * 0.125, qst_f, qxf)
    m_qf.start()
    gather_b.near()
    gather_f.start_y()
    m_do.wait_recv()
    turned = dox[...].astype(F32).T.astype(BF16)
    nothing = jnp.zeros((CHIP, 64), F32)
    for h in range(4):
        cols = pl.ds(h * CHIP, CHIP)
        wd[0:64, cols] = jnp.zeros((64, CHIP), BF16)
        wd[64:128, cols] = turned[h * 64:(h + 1) * 64, :]
        head_q = qxb[:, h * 64:(h + 1) * 64].astype(F32)
        head_o = dox[:, h * 64:(h + 1) * 64].astype(F32)
        wkq[cols, :] = jnp.concatenate([head_q, nothing], axis=1).astype(BF16)
        wvo[cols, :] = jnp.concatenate([nothing, head_o], axis=1).astype(BF16)
    m_qf.wait_recv()
    query_operand(qxf, ws_f)

    PS, SS = (pa, pb), (sa, sb)

    def keys_of(kv, block):
        d, half = block
        return kv[d, 2 * half:2 * half + 2].reshape(KB, 128)

    def attention(kv, ws, hooks):
        acc[...] = jnp.zeros_like(acc)
        maxima = []
        lane = lax.broadcasted_iota(jnp.int32, (KB, 128), 1)
        for t in range(10):
            if t in hooks:
                hooks[t]()
            if t < 8:
                operand = jnp.concatenate(
                    [keys_of(kv, FORWARD_ORDER[t]), keys_of(aux, FORWARD_ORDER[t])], axis=1
                )
                tops = []
                for r in range(4):
                    cols = pl.ds(r * CHIP, CHIP)
                    scores = dot(operand, ws[:, cols], NN)
                    SS[t % 2][:, cols] = scores
                    tops.append(jnp.max(scores.reshape(KB // 8, 8, CHIP), axis=0))
                top = jnp.max(jnp.concatenate(tops, axis=1), axis=0, keepdims=True)
                before = maxima[-1] if maxima else jnp.full((1, QROWS), FIRST_MAX, F32)
                maxima.append(jnp.maximum(before, top))
                mrow[t:t + 1, :] = maxima[-1]
            if 1 <= t <= 8:
                n = t - 1
                for r in range(4):
                    cols = pl.ds(r * CHIP, CHIP)
                    PS[n % 2][n // 2, :, cols] = jnp.exp(
                        SS[n % 2][:, cols] - maxima[n][:, r * CHIP:(r + 1) * CHIP]
                    ).astype(BF16)
            if t >= 2:
                n = t - 2
                block = keys_of(kv, FORWARD_ORDER[n])
                turned = jnp.where(lane < 64, jnp.ones_like(block), block).T
                term = dot(turned, PS[n % 2][n // 2], NN)
                if n == 0:
                    acc[...] = term
                else:
                    acc[...] = acc[...] * jnp.exp(maxima[n - 1] - maxima[n]) + term
        return maxima[-1]

    def tokens_first(columns, staged, whole):
        tall = jnp.concatenate([columns[:, h * CHIP:(h + 1) * CHIP] for h in range(4)], axis=0)
        rows = tall.T.astype(BF16)
        staged[0] = rows[0:128]
        staged[1] = rows[128:256]
        whole[core] = staged[core]

    def second_row():
        gather_b.middle()
        gather_b.forward(1)
        gather_f.forward(0)

    def last_b():
        gather_b.wait_far(1)
        gather_f.near()

    final_max = attention(
        kvb, ws_b,
        {
            1: lambda: gather_b.wait_far(0),
            2: second_row,
            3: lambda: gather_b.forward(3),
            4: lambda: gather_b.wait_x(2),
            5: lambda: gather_b.wait_far(2),
            6: last_b,
            7: lambda: gather_b.wait_far(3),
            8: gather_f.middle,
        },
    )
    inverse_sum = 1.0 / acc[0:1, :]
    attended = (acc[64:128, :] * inverse_sum).astype(BF16).astype(F32)
    delta = jnp.sum(wd[64:128, :].astype(F32) * attended, axis=0, keepdims=True)
    frow[...] = jnp.exp(mrow[...] - final_max) * inverse_sum

    def add_x(d):
        whole = d0[d]
        for p in (1, 2, 3):
            sum_x[(d, p)].wait_recv()
            whole = whole + rx[d, p - 1].astype(F32)
        dkv[d, 0] = whole.astype(BF16)
        sum_y[d].start()

    TS, US = (ta, tb), (ua, ub)
    accq[...] = jnp.zeros_like(accq)

    for t in range(9):
        if t == 4:
            gather_f.forward(1)
        if t == 5:
            gather_f.forward(3)
        if t == 8:
            add_x(2)
        if t < 8:
            n = FORWARD_ORDER.index(BACKWARD_ORDER[t])
            keys = keys_of(kvb, BACKWARD_ORDER[t])
            for r in range(4):
                cols = pl.ds(r * CHIP, CHIP)
                grads = dot(keys, wd[:, cols], NN) - delta[:, r * CHIP:(r + 1) * CHIP]
                prob = PS[n % 2][n // 2, :, cols].astype(F32) * frow[n:n + 1, cols]
                TS[t % 2][:, cols] = prob.astype(BF16)
                US[t % 2][:, cols] = (prob * grads).astype(BF16)
        if t >= 1:
            d, half = BACKWARD_ORDER[t - 1]
            score_grads = US[(t - 1) % 2][...]
            accq[...] += dot(keys_of(kvb, (d, half)).T, score_grads, NN)
            terms = dot(score_grads, wkq[...], NN) + dot(TS[(t - 1) % 2][...], wvo[...], NN)
            if half == 0:
                d0[d] = terms[0:CHIP]
                dkv[d, 1] = terms[CHIP:].astype(BF16)
                sum_x[(d, 1)].start()
            else:
                dkv[d, 2] = terms[0:CHIP].astype(BF16)
                dkv[d, 3] = terms[CHIP:].astype(BF16)
                sum_x[(d, 3)].start()
                sum_x[(d, 2)].start()

    tokens_first(accq[0:64, :] * 0.125, dqst, dqx)
    m_dq.start()

    def query_part():
        m_dq.wait_recv()
        part[...] = dot(jnp.concatenate([dqx[0], dqx[1]], axis=1), wq[...], NT)

    def add_own_x():
        whole = d0[0]
        for p in (1, 2, 3):
            sum_x[(0, p)].wait_recv()
            whole = whole + rx[0, p - 1].astype(F32)
        d0[0] = whole

    def sum_own():
        whole = d0[0]
        for d in (1, 3, 2):
            sum_y[d].wait_recv()
            whole = whole + ry[d - 1].astype(F32)
        whole = whole.astype(BF16)
        dfst[0] = whole[0:128]
        dfst[1] = whole[128:256]
        dfin[core] = dfst[core]
        m_dkv.start()

    def finish_backward():
        m_dkv.wait_recv()
        first, second = dfin[0].astype(F32), dfin[1].astype(F32)
        key_value = jnp.concatenate(
            [first[:, 0:64], second[:, 0:64], first[:, 64:128], second[:, 64:128]], axis=1
        ).astype(BF16)
        for h in range(2):
            rows = pl.ds(64 * h, 64)
            grads = part[rows, :] + dot(key_value[64 * h:64 * h + 64], wkv[...], NT)
            scaled = grads * gain[...]
            wide = xb[rows, :].astype(F32)
            inverse = lax.rsqrt(jnp.mean(wide * wide, axis=-1, keepdims=True) + NORM_EPSILON)
            mean = jnp.mean(wide * scaled, axis=-1, keepdims=True)
            stage_b[rows, :] = (
                cot[rows, :].astype(F32) + inverse * scaled
                - wide * (inverse * inverse * inverse) * mean
            ).astype(BF16)
            m_out_b[h].start()

    attention(
        kvf, ws_f,
        {
            1: lambda: (gather_f.wait_far(0), add_x(1)),
            3: lambda: add_x(3),
            4: lambda: gather_f.wait_x(2),
            5: lambda: gather_f.wait_far(2),
            6: lambda: gather_f.wait_far(1),
            7: lambda: (gather_f.wait_far(3), query_part()),
            9: add_own_x,
        },
    )
    tokens_first(acc[64:128, :] * (1.0 / acc[0:1, :]), ost, att)
    m_att.start()
    m_att.wait_recv()
    attended = jnp.concatenate([att[0], att[1]], axis=1)
    for h in range(2):
        cols = pl.ds(512 * h, 512)
        stage_f[:, cols] = (
            xf[:, cols].astype(F32) + dot(attended, wo[:, cols], NN)
        ).astype(BF16)
        m_out_f[h].start()
        if h == 0:
            sum_own()
    finish_backward()
    for copy in used:
        copy.wait_send()
    for copy in m_out_f + m_out_b:
        copy.wait_recv()


def hand_over(in_f, in_b, out_f, out_b, held, in_sem, out_sem):
    pieces = []
    for i, (src, dst) in enumerate(((in_f, out_f), (in_b, out_b))):
        for h in range(2):
            rows = pl.ds(64 * h, 64)
            arrive = pltpu.make_async_copy(src.at[rows], held.at[i, rows], in_sem.at[2 * i + h])
            leave = pltpu.make_async_copy(held.at[i, rows], dst.at[rows], out_sem.at[2 * i + h])
            arrive.start()
            pieces.append((arrive, leave))
    for arrive, leave in pieces:
        arrive.wait()
        leave.start()
    for _, leave in pieces:
        leave.wait()


def on_device(
    forward_input, stored_input, output_cotangent, norm_gain,
    query_weight, key_weight, value_weight, output_weight, frame_index, valid_counts,
):
    any_space = pl.BlockSpec(memory_space=pl.ANY)
    vmem = pl.BlockSpec(memory_space=pltpu.VMEM)
    shape = jax.ShapeDtypeStruct((ROWS, D), BF16)
    scratch = [
        (ROWS, D), (ROWS, D), (ROWS, D), (D, 512), (D, 256), (512, D), (ROWS, D),
        (2, ROWS, 128), (2, ROWS, 128), (4, 4, CHIP, 128), (4, 4, CHIP, 128), (4, 4, CHIP, 128),
        (2, ROWS, 256), (2, ROWS, 256), (2, ROWS, 256), (CHIP, 256), (CHIP, 256), (CHIP, 256),
        (256, QROWS), (256, QROWS), (128, QROWS), (QROWS, 128), (QROWS, 128),
        (4, KB, QROWS), (4, KB, QROWS), ((KB, QROWS), F32), ((KB, QROWS), F32),
        (KB, QROWS), (KB, QROWS), (KB, QROWS), (KB, QROWS),
        ((128, QROWS), F32), ((128, QROWS), F32), ((8, QROWS), F32), ((8, QROWS), F32),
        (4, 4, CHIP, 128), ((4, CHIP, 128), F32), (4, 3, CHIP, 128), (3, CHIP, 128),
        (2, ROWS, 128), (2, ROWS, 128), ((ROWS, D), F32),
        (2, ROWS, 256), (2, ROWS, 256), (2, ROWS, 256), (2, ROWS, 256), (ROWS, D), (ROWS, D),
    ]
    scratch = [
        pltpu.VMEM(*s) if isinstance(s[1], type) or not isinstance(s[1], int) else pltpu.VMEM(s, BF16)
        for s in scratch
    ]
    out_f, out_b = pl.pallas_call(
        fused,
        out_shape=(shape, shape),
        in_specs=[any_space] * 3 + [vmem] + [any_space] * 4
        + [vmem, pl.BlockSpec(memory_space=pltpu.SMEM)],
        out_specs=(any_space, any_space),
        scratch_shapes=scratch + [
            pltpu.SemaphoreType.DMA((7,)),
            pltpu.SemaphoreType.DMA((MESSAGES,)),
            pltpu.SemaphoreType.DMA((MESSAGES,)),
        ],
        compiler_params=pltpu.CompilerParams(
            collective_id=0, has_side_effects=True, vmem_limit_bytes=56 * 2**20
        ),
        name="sublayer",
    )(
        forward_input[0], stored_input[0], output_cotangent[0], norm_gain,
        query_weight[0], key_weight[0], value_weight[0], output_weight[0],
        frame_index.reshape(32, 128), valid_counts,
    )
    out_f, out_b = pl.pallas_call(
        hand_over,
        out_shape=(shape, shape),
        in_specs=[any_space] * 2,
        out_specs=(any_space, any_space),
        scratch_shapes=[
            pltpu.VMEM((2, ROWS, D), BF16), pltpu.SemaphoreType.DMA((4,)), pltpu.SemaphoreType.DMA((4,)),
        ],
        name="hand_over",
    )(out_f, out_b)
    return out_f[None], out_b[None]


def solution(mesh):
    return jax.shard_map(
        on_device,
        mesh=mesh,
        in_specs=(
            P("section", "seq", None),
            P("section", "seq", None),
            P("section", "seq", None),
            P("section", None),
            P("section", None, None),
            P("section", None, None),
            P("section", None, None),
            P("section", None, None),
            P(),
            P(),
        ),
        out_specs=(P("section", "seq", None), P("section", "seq", None)),
        check_vma=False,
    )
```
